256 devices in a mesh: rows: 64 (over y, x, z_lo, core), feat: 4 (over z_hi).
Axes of the slice: x: 4, y: 4, z: 8 (z_hi: 4, z_lo: 2; z = z_hi * 2 + z_lo), core: 2. Of those that a mesh axis runs over, the one named last changes fastest.
Arguments:
- cells: bfloat16 [4096, 128, 192], P('rows', 'feat'), may hold values from -6 to 6
- labels: int32 [4096], P('rows'), may hold values from 0 to 1, as said below
- missing: int32 [4096, 128], P('rows', 'feat'), may hold values 0 or 1
- feat_qkv: bfloat16 [192, 576], replicated, may hold values from -16 to 16
- feat_out: bfloat16 [192, 192], replicated, may hold values from -0.4375 to 0.4375
- gain_feat: float32 [192], replicated, may hold values from 0.25 to 1.75
- row_q: bfloat16 [192, 192], replicated, may hold values from -16 to 16
- row_kv: bfloat16 [192, 384], replicated, may hold values from -0.4375 to 0.4375
- row_out: bfloat16 [192, 192], replicated, may hold values from -0.4375 to 0.4375
- gain_row: float32 [192], replicated, may hold values from 0.25 to 1.75
- mlp_in: bfloat16 [192, 384], replicated, may hold values from -0.4375 to 0.4375
- mlp_out: bfloat16 [384, 192], replicated, may hold values from -0.3125 to 0.3125
- gain_mlp: float32 [192], replicated, may hold values from 0.25 to 1.75
Outputs:
- cells_out: bfloat16 [4096, 128, 192], P('rows', 'feat')
The draws below stay inside these ranges and needn't reach their ends.
Inputs may be any that keep to these rules, and one draw needn't show every extreme that they name: `labels`: 1 marks a training row; each aligned block of 64 rows holds between 4 and 8 training rows, and some block holds exactly 8.
All inputs are finite; a program needn't handle non-finite values. No bound on the sum of `missing` on one device may be relied on, other than what follows from the above.
Results may differ from the reference program's by a relative error of at most 0.02.
The reference program's roundings to bfloat16 on the way count: a program that leaves them out, or rounds other values in their place, can miss the bound.
Values may be sent and summed in bfloat16 or wider, within the bound.
No kernel may reach another device: no remote copies, remote signals or barrier semaphores. Data moves between devices by JAX's collectives and lax.ppermute only.
A program may use at most 320 MiB of HBM per device.

```python
import math
import jax
import jax.numpy as jnp
from jax import lax

EMB = 192
HEADS = 6
HID = 384
FEAT = 128
ROW_DEV = 64
TRAIN_MOST = 8
ROWS = 4096


def boosted_weight(key, rows, cols, strong, weak):
    normal_part = jnp.clip(jax.random.normal(key, (rows, cols), jnp.float32), -3.0, 3.0) / math.sqrt(rows)
    first_head = jax.random.randint(jax.random.fold_in(key, 5), (), 0, HEADS)
    other_head = (first_head + 1 + jax.random.randint(jax.random.fold_in(key, 6), (), 0, HEADS - 1)) % HEADS
    columns = jnp.arange(cols) // (EMB // HEADS)
    head_factor = jnp.where(columns == first_head, strong, jnp.where(columns == other_head, weak, 1.0))
    return jnp.clip(normal_part * head_factor[None, :], -16.0, 16.0)


def draw_labels(key, part):
    key = jax.random.fold_in(key, 3)
    block_count = ROWS // ROW_DEV
    lowest = max(1, TRAIN_MOST // 2)
    counts = jax.random.randint(jax.random.fold_in(key, 1), (block_count,), lowest, TRAIN_MOST + 1)
    fullest = jax.random.randint(jax.random.fold_in(key, 2), (), 0, block_count)
    counts = jnp.where(jnp.arange(block_count) == fullest, TRAIN_MOST, counts)
    block_keys = jax.random.split(jax.random.fold_in(key, 4), block_count)
    orders = jax.vmap(lambda single: jax.random.permutation(single, ROW_DEV))(block_keys)
    return (orders < counts[:, None]).astype(jnp.int32).reshape(ROWS)


def draw_feat_qkv(key, part):
    key = jax.random.fold_in(key, 11)
    return boosted_weight(key, EMB, 3 * EMB, 1.0, 1.0).astype(jnp.bfloat16)


def draw_row_q(key, part):
    key = jax.random.fold_in(key, 13)
    return boosted_weight(key, EMB, EMB, 1.0, 1.0).astype(jnp.bfloat16)


def plant(entries, own_key, smallest, top_value):
    spot = [jax.random.randint(jax.random.fold_in(own_key, axis), (), 0, length) for axis, length in enumerate(entries.shape)]
    main_axis = entries.shape.index(max(entries.shape))
    neighbour = spot[:main_axis] + [(spot[main_axis] + 1) % entries.shape[main_axis]] + spot[main_axis + 1:]
    return entries.at[tuple(spot)].set(smallest).at[tuple(neighbour)].set(top_value)


def steps_of(key, shape, shards, least, largest):
    factor_of, own = 1.0, jax.random.fold_in(key, 6)
    for position, blocks in shards:
        heights = jnp.exp(jax.random.uniform(jax.random.fold_in(own, position), (blocks,), jnp.float32, least / len(shards), largest / len(shards)))
        factor_of = factor_of * jnp.repeat(heights, shape[position] // blocks).reshape([-1 if axis == position else 1 for axis in range(len(shape))])
    return factor_of


def noise(own_key, dims, spread, reach, cuts=(), held_as=jnp.bfloat16):
    drawn = jax.random.normal(own_key, dims, jnp.float32) * spread
    if len(cuts) > 0:
        drawn = steps_of(own_key, dims, cuts, -0.22, 0.18) * drawn
    return jnp.clip(drawn, min=-reach, max=reach).astype(held_as)


def setup_inputs(seed: int = 0) -> dict:
    arg_keys = jax.random.split(jax.random.key(seed), 14)
    return {
        "cells": noise(arg_keys[0], (ROWS, FEAT, EMB), 1.0, 6.0, ((0, 64), (1, 4))),
        "labels": draw_labels(jax.random.fold_in(arg_keys[13], 71), 0),
        "missing": plant((jax.random.randint(arg_keys[2], (ROWS, FEAT), 0, 4) < 1).astype(jnp.int32), jax.random.fold_in(arg_keys[2], 1), 0, 1),
        "feat_qkv": draw_feat_qkv(jax.random.fold_in(arg_keys[13], 71), 0),
        "feat_out": noise(arg_keys[4], (EMB, EMB), EMB ** -0.5, 0.4375),
        "gain_feat": jnp.clip(1.0 + 0.15 * jax.random.normal(arg_keys[5], (EMB,), jnp.float32), 0.25, 1.75),
        "row_q": draw_row_q(jax.random.fold_in(arg_keys[13], 71), 0),
        "row_kv": noise(arg_keys[7], (EMB, 2 * EMB), EMB ** -0.5, 0.4375),
        "row_out": noise(arg_keys[8], (EMB, EMB), EMB ** -0.5, 0.4375),
        "gain_row": jnp.clip(1.0 + 0.15 * jax.random.normal(arg_keys[9], (EMB,), jnp.float32), 0.25, 1.75),
        "mlp_in": noise(arg_keys[10], (EMB, HID), EMB ** -0.5, 0.4375),
        "mlp_out": noise(arg_keys[11], (HID, EMB), HID ** -0.5, 0.3125),
        "gain_mlp": jnp.clip(1.0 + 0.15 * jax.random.normal(arg_keys[12], (EMB,), jnp.float32), 0.25, 1.75),
    }


EPSILON = 1e-05

def rounded(values):
    return lax.optimization_barrier(values.astype(jnp.bfloat16))

def layer_norm(values, gain):
    average = lax.optimization_barrier(jnp.mean(values, axis=-1, keepdims=True))
    centred = values - average
    variance = lax.optimization_barrier(jnp.mean(centred * centred, axis=-1, keepdims=True))
    return centred * lax.rsqrt(variance + EPSILON) * gain

def feature_block(block_cells, block_missing, feat_qkv, feat_out, gain_feat):
    row_count, feats, width = block_cells.shape
    head_size = width // HEADS
    packed = jnp.dot(block_cells.reshape(row_count * feats, width), feat_qkv, preferred_element_type=jnp.float32)
    packed = rounded(packed).astype(jnp.float32).reshape(row_count, feats, 3, HEADS, head_size)
    scores = jnp.einsum('bihd,bjhd->bhij', packed[:, :, 0], packed[:, :, 1]) / math.sqrt(head_size)
    diagonal = jnp.eye(feats, dtype=bool)
    allowed = (block_missing[:, None, None, :] == 0) | diagonal[None, None]
    scores = jnp.where(allowed, scores, -jnp.inf)
    highest = lax.optimization_barrier(jnp.max(scores, axis=-1, keepdims=True))
    weights = jnp.exp(scores - highest)
    summed = lax.optimization_barrier(jnp.sum(weights, axis=-1))
    probabilities = rounded(weights).astype(jnp.float32)
    attended = jnp.einsum('bhij,bjhd->bihd', probabilities, packed[:, :, 2])
    attended = attended / jnp.transpose(summed, (0, 2, 1))[..., None]
    attended = attended.astype(jnp.bfloat16).reshape(row_count * feats, width)
    update = jnp.dot(attended, feat_out, preferred_element_type=jnp.float32)
    merged = block_cells.reshape(row_count * feats, width).astype(jnp.float32) + update
    return layer_norm(merged, gain_feat).astype(jnp.bfloat16).reshape(row_count, feats, width)

def compact_rows(block_cells, block_labels):
    row_count = block_cells.shape[0]
    slot_index = (jnp.cumsum(block_labels) - 1).astype(jnp.int32)
    positions = jnp.arange(TRAIN_MOST, dtype=jnp.int32)
    select = ((slot_index[None, :] == positions[:, None]) & (block_labels[None, :] == 1)).astype(jnp.bfloat16)
    chosen = jnp.dot(select, block_cells.reshape(row_count, -1), preferred_element_type=jnp.float32)
    occupied = positions < jnp.sum(block_labels).astype(jnp.int32)
    return (chosen.astype(jnp.bfloat16), occupied)

def reference(cells, labels, missing, feat_qkv, feat_out, gain_feat, row_q, row_kv, row_out, gain_row, mlp_in, mlp_out, gain_mlp):
    block_count = ROWS // ROW_DEV
    head_size = EMB // HEADS

    def feature_step(operands):
        return feature_block(operands[0], operands[1], feat_qkv, feat_out, gain_feat)
    after_features = lax.map(feature_step, (cells.reshape(block_count, ROW_DEV, FEAT, EMB), missing.reshape(block_count, ROW_DEV, FEAT)))

    def compact_step(operands):
        return compact_rows(operands[0], operands[1])
    chosen, occupied = lax.map(compact_step, (after_features, labels.reshape(block_count, ROW_DEV)))
    occupied = occupied.reshape(-1)
    keyvals = jnp.dot(chosen.reshape(-1, EMB), row_kv, preferred_element_type=jnp.float32)
    keyvals = rounded(keyvals).astype(jnp.float32).reshape(block_count * TRAIN_MOST, FEAT, 2, HEADS, head_size)
    key_part = keyvals[:, :, 0]
    value_part = keyvals[:, :, 1]

    def row_step(block_rows):
        row_count = block_rows.shape[0]
        flattened = block_rows.reshape(-1, EMB)
        queries = rounded(jnp.dot(flattened, row_q, preferred_element_type=jnp.float32)).astype(jnp.float32)
        queries = queries.reshape(row_count, FEAT, HEADS, head_size)
        scores = jnp.einsum('rfhd,tfhd->rfht', queries, key_part) / math.sqrt(head_size)
        scores = jnp.where(occupied[None, None, None, :], scores, -jnp.inf)
        highest = lax.optimization_barrier(jnp.max(scores, axis=-1, keepdims=True))
        weights = jnp.exp(scores - highest)
        summed = lax.optimization_barrier(jnp.sum(weights, axis=-1))
        probabilities = rounded(weights).astype(jnp.float32)
        attended = jnp.einsum('rfht,tfhd->rfhd', probabilities, value_part) / summed[..., None]
        attended = attended.astype(jnp.bfloat16).reshape(-1, EMB)
        merged = flattened.astype(jnp.float32) + jnp.dot(attended, row_out, preferred_element_type=jnp.float32)
        after_rows = layer_norm(merged, gain_row).astype(jnp.bfloat16)
        hidden = jax.nn.gelu(jnp.dot(after_rows, mlp_in, preferred_element_type=jnp.float32)).astype(jnp.bfloat16)
        combined = after_rows.astype(jnp.float32) + jnp.dot(hidden, mlp_out, preferred_element_type=jnp.float32)
        return layer_norm(combined, gain_mlp).astype(jnp.bfloat16).reshape(row_count, FEAT, EMB)
    result = lax.map(row_step, after_features.reshape(ROWS // 8, 8, FEAT, EMB))
    return result.reshape(ROWS, FEAT, EMB)
```

```python
import functools
import math

import jax
import jax.numpy as jnp
from jax import lax
from jax.experimental import pallas as pl
from jax.experimental.pallas import tpu as pltpu
from jax.sharding import PartitionSpec as P

HEADS = 6
HEAD = 32
WIDTH = 192
TAIL = WIDTH - 128
TRAIN_MOST = 8
EPSILON = 1e-05
BF = jnp.bfloat16
F32 = jnp.float32
NEVER = -1e30
SCALE = math.log2(math.e) / math.sqrt(HEAD)
VMEM = pl.BlockSpec(memory_space=pltpu.VMEM)
SMEM = pl.BlockSpec(memory_space=pltpu.SMEM)


def mm(a, b):
    return lax.dot_general(a, b, (((1,), (0,)), ((), ())), preferred_element_type=F32)


def mm_nt(a, b):
    return lax.dot_general(a, b, (((1,), (1,)), ((), ())), preferred_element_type=F32)


def mm_tn(a, b):
    return lax.dot_general(a, b, (((0,), (0,)), ((), ())), preferred_element_type=F32)


def layer_norm(values, gain):
    average = jnp.mean(values, axis=-1, keepdims=True)
    centred = values - average
    variance = jnp.mean(centred * centred, axis=-1, keepdims=True)
    return centred * lax.rsqrt(variance + EPSILON) * gain


def turned(w):
    return jnp.transpose(w.astype(F32)).astype(BF)


def params(flops, size, exps=0):
    return dict(
        compiler_params=pltpu.CompilerParams(vmem_limit_bytes=56 * 2**20),
        cost_estimate=pl.CostEstimate(flops=flops, bytes_accessed=size, transcendentals=exps),
    )


def halves(tail, part):
    return tail[:, part * TAIL : (part + 1) * TAIL]


def prepare_kernel(rows_dev, feats, cells, labels, missing, out0, out1, out2, out3, train, picked, flags):
    me = lax.axis_index("feat")
    share = rows_dev // 4
    count = share * feats
    for k, out in enumerate((out0, out1, out2, out3)):
        start = lax.rem(me + k, 4) * share
        x = cells[pl.ds(start, share)].reshape(count, WIDTH)
        out[0:count, :] = x[:, :128]
        out[count : count + count // 2, 0:TAIL] = x[: count // 2, 128:]
        out[count : count + count // 2, TAIL:128] = x[count // 2 :, 128:]
        out[count * 3 // 2 :, :] = jnp.zeros((share, 128), BF)
        out[count * 3 // 2 :, 0:feats] = missing[pl.ds(start, share), :].astype(F32).astype(BF)
    picked[...] = jnp.zeros(picked.shape, BF)
    flags[...] = jnp.zeros(flags.shape, F32)

    def step(r, slot):
        is_train = labels[r] == 1

        @pl.when(is_train)
        def _():
            picked[slot] = cells[r]
            flags[pl.ds(slot, 1), 0:feats] = missing[pl.ds(r, 1), :].astype(F32)

        return jnp.minimum(slot + is_train.astype(jnp.int32), TRAIN_MOST - 1)

    lax.fori_loop(0, rows_dev, step, jnp.int32(0))
    count = TRAIN_MOST * feats
    x = picked[...].reshape(count, WIDTH)
    train[0:count, :] = x[:, :128]
    train[count : count + count // 2, 0:TAIL] = x[: count // 2, 128:]
    train[count : count + count // 2, TAIL:128] = x[count // 2 :, 128:]
    train[count * 3 // 2 :, :] = flags[...].astype(BF)


def feature_rows(pieces, rows, feats, weights, scratch, keep, emit):
    feat_qkv, feat_out, gain_feat = weights
    turned_qv, blocks = scratch
    all_feats = 4 * feats
    turned_qv[0:WIDTH, :] = turned(feat_qkv[:, 0:WIDTH])
    turned_qv[WIDTH : 2 * WIDTH, :] = turned(feat_qkv[:, 2 * WIDTH : 3 * WIDTH])
    blocks[...] = jnp.zeros(blocks.shape, BF)
    count = rows * feats
    flags = jnp.concatenate([p[count * 3 // 2 :, 0:feats].astype(F32) for p in pieces], axis=1)
    flags = jnp.concatenate(
        [flags, jnp.zeros((128 - flags.shape[0], all_feats), F32)], axis=0
    )
    flags = jnp.transpose(flags)
    same = lax.broadcasted_iota(jnp.int32, (all_feats, all_feats), 0) == lax.broadcasted_iota(
        jnp.int32, (all_feats, all_feats), 1
    )
    gain = gain_feat[...]
    for r in range(rows // 2):
        pair = []
        for part in range(2):
            row = r + part * (rows // 2)
            pair.extend(
                jnp.concatenate(
                    [
                        p[row * feats : (row + 1) * feats, :],
                        halves(p[count + r * feats : count + (r + 1) * feats, :], part),
                    ],
                    axis=1,
                )
                for p in pieces
            )
        x = jnp.concatenate(pair, axis=0)
        keys = mm(x, feat_qkv[:, WIDTH : 2 * WIDTH]).astype(BF)
        turned_q_v = mm_nt(turned_qv[...], x).astype(BF)
        for part in range(2):
            row = r + part * (rows // 2)
            lanes = slice(part * all_feats, (part + 1) * all_feats)
            spot = blocks.at[part]
            for h in range(HEADS):
                spot[h * HEAD : (h + 1) * HEAD, h * 128 : h * 128 + 128] = turned_q_v[
                    h * HEAD : (h + 1) * HEAD, lanes
                ]
            allowed = (flags[:, row : row + 1] == 0) | same
            attended = []
            for g in range(HEADS // 2):
                scores = mm(keys[lanes, :], spot[:, g * 256 : (g + 1) * 256])
                scores = jnp.concatenate(
                    [jnp.where(allowed, scores[:, i * 128 : (i + 1) * 128], NEVER) for i in range(2)],
                    axis=1,
                )
                highest = jnp.max(scores, axis=0, keepdims=True)
                exps = jnp.exp2((scores - highest) * SCALE)
                total = jnp.sum(exps, axis=0, keepdims=True)
                mixed = mm(
                    turned_q_v[WIDTH + g * 64 : WIDTH + (g + 1) * 64, lanes], exps.astype(BF)
                )
                attended.append((mixed[0:HEAD, 0:128] / total[:, 0:128]).astype(BF))
                attended.append((mixed[HEAD:64, 128:256] / total[:, 128:256]).astype(BF))
            attended = jnp.concatenate(attended, axis=0)
            update = mm_tn(attended, feat_out[...])[0:keep]
            merged = x[part * all_feats : part * all_feats + keep].astype(F32) + update
            emit(row, layer_norm(merged, gain))


def train_kernel(
    feats, p0, p1, p2, p3, labels, feat_qkv, feat_out, gain_feat, mine, other, turned_qv, blocks, heads, tails
):
    core = lax.rem(lax.axis_index("rows"), 2)

    def emit(row, y):
        heads[pl.ds(row, feats, stride=TRAIN_MOST), :] = y[:, :128]
        tails[pl.ds(row, feats, stride=TRAIN_MOST), :] = jnp.concatenate([y[:, 128:], y[:, 128:]], axis=1)

    feature_rows(
        (p0, p1, p2, p3), TRAIN_MOST, feats, (feat_qkv, feat_out, gain_feat), (turned_qv, blocks), feats, emit
    )
    count = feats // 2 * TRAIN_MOST
    trained = jnp.sum(labels[...], axis=1, keepdims=True)
    bias = jnp.where(lax.broadcasted_iota(jnp.int32, (16, 128), 0) < trained, 0.0, NEVER)
    for rel, out in enumerate((mine, other)):
        base = jnp.where(rel == 0, core, 1 - core) * count
        out[0:count, :] = heads[pl.ds(base, count), :].astype(BF)
        first = tails[pl.ds(base, count // 2), 0:TAIL]
        second = tails[pl.ds(base + count // 2, count // 2), TAIL:128]
        out[count : count * 3 // 2, :] = jnp.concatenate([first, second], axis=1).astype(BF)
        out[count * 3 // 2 :, :] = bias.astype(BF)


def merge_kernel(feats, a, b, c, d, out):
    count = feats * TRAIN_MOST
    parts = [p[...].astype(F32) for p in (a, b, c, d)]

    def side(start, groups):
        joined = jnp.concatenate(
            [p[start : start + groups * 8].reshape(groups, 8, 128) for p in parts], axis=1
        )
        return joined.reshape(groups * 32, 128).astype(BF)

    out[0 : 4 * count, :] = side(0, feats)
    out[4 * count : 6 * count, :] = side(count, feats // 2)
    out[6 * count :, :] = side(count * 3 // 2, 1)


def feature_kernel(
    rows,
    feats,
    p0,
    p1,
    p2,
    p3,
    feat_qkv,
    feat_out,
    gain_feat,
    *rest,
):
    outs, (turned_qv, blocks, heads, tails) = rest[:8], rest[8:]
    core = lax.rem(lax.axis_index("rows"), 2)

    def emit(row, y):
        heads[pl.ds(row, 4 * feats, stride=rows), :] = y[:, :128]
        tails[pl.ds(row, 4 * feats, stride=rows), :] = jnp.concatenate([y[:, 128:], y[:, 128:]], axis=1)

    feature_rows(
        (p0, p1, p2, p3), rows, feats, (feat_qkv, feat_out, gain_feat), (turned_qv, blocks), 4 * feats, emit
    )
    count = feats // 2 * rows
    for k in range(4):
        for rel in range(2):
            base = (2 * k + jnp.where(rel == 0, core, 1 - core)) * count
            out = outs[2 * k + rel]
            out[0:count, :] = heads[pl.ds(base, count), :].astype(BF)
            first = tails[pl.ds(base, count // 2), 0:TAIL]
            second = tails[pl.ds(base + count // 2, count // 2), TAIL:128]
            out[count:, :] = jnp.concatenate([first, second], axis=1).astype(BF)


def row_kernel(feats, share, train_each, *refs):
    trains, chunks = refs[0:4], refs[4:12]
    row_q, row_kv, row_out, gain_row, mlp_in, mlp_out, gain_mlp = refs[12:19]
    mine, other = refs[19:21]
    turned_q, turned_v, blocks, train_cells, row_cells, bias, heads, tails = refs[21:]
    rows = share * len(chunks)
    piece = feats * train_each * 3 // 2 + train_each
    lines = trains[0].shape[0] // piece
    keys_all = 4 * lines * train_each
    turned_q[...] = turned(row_q[...])
    turned_v[...] = turned(row_kv[:, WIDTH : 2 * WIDTH])
    blocks[...] = jnp.zeros(blocks.shape, BF)
    blocks[:, WIDTH : WIDTH + 16, :] = jnp.where(
        lax.broadcasted_iota(jnp.int32, (2, 16, HEADS * 128), 1) == 0, 1.0, 0.0
    ).astype(BF)
    for n in range(4):
        for line in range(lines):
            spot = (n * lines + line) * train_each
            bias[spot : spot + train_each, :] = trains[n][
                line * piece + feats * train_each * 3 // 2 : (line + 1) * piece, 0:TAIL
            ]

    def pair(j, carry):
        for n in range(4):
            for line in range(lines):
                spot = slice((n * lines + line) * train_each, (n * lines + line + 1) * train_each)
                base = line * piece
                tail = trains[n][
                    pl.ds(base + feats * train_each + j * train_each, train_each), :
                ]
                for part in range(2):
                    train_cells[part, spot, 0:128] = trains[n][
                        pl.ds(base + (j + part * (feats // 2)) * train_each, train_each), :
                    ]
                    train_cells[part, spot, 128:WIDTH] = halves(tail, part)
        for n, chunk in enumerate(chunks):
            tail = chunk[pl.ds(feats * share + j * share, share), :]
            for part in range(2):
                spot = slice(part * rows + n * share, part * rows + (n + 1) * share)
                row_cells[spot, 0:128] = chunk[pl.ds((j + part * (feats // 2)) * share, share), :]
                row_cells[spot, 128:WIDTH] = halves(tail, part)
        x = row_cells[...]
        turned_queries = mm_nt(turned_q[...], x).astype(BF)
        updates = []
        for part in range(2):
            cells = train_cells[part]
            keys = jnp.concatenate([mm(cells, row_kv[:, 0:WIDTH]).astype(BF), bias[...]], axis=1)
            values = mm_nt(turned_v[...], cells).astype(BF)
            spot = blocks.at[part]
            for h in range(HEADS):
                spot[h * HEAD : (h + 1) * HEAD, h * 128 : h * 128 + 128] = turned_queries[
                    h * HEAD : (h + 1) * HEAD, part * rows : (part + 1) * rows
                ]
            attended = []
            for g in range(HEADS // 2):
                scores = mm(keys, spot[:, g * 256 : (g + 1) * 256])
                highest = jnp.max(scores, axis=0, keepdims=True)
                exps = jnp.exp2((scores - highest) * SCALE)
                total = jnp.sum(exps, axis=0, keepdims=True)
                mixed = mm(values[g * 64 : (g + 1) * 64, :], exps.astype(BF))
                attended.append((mixed[0:HEAD, 0:128] / total[:, 0:128]).astype(BF))
                attended.append((mixed[HEAD:64, 128:256] / total[:, 128:256]).astype(BF))
            updates.append(mm_tn(jnp.concatenate(attended, axis=0), row_out[...]))
        merged = x.astype(F32) + jnp.concatenate(updates, axis=0)
        after_rows = layer_norm(merged, gain_row[...]).astype(BF)
        hidden = jax.nn.gelu(mm(after_rows, mlp_in[...])).astype(BF)
        combined = after_rows.astype(F32) + mm(hidden, mlp_out[...])
        y = layer_norm(combined, gain_mlp[...])
        for part in range(2):
            own = y[part * rows : (part + 1) * rows]
            spot = pl.ds(j + part * (feats // 2), rows, stride=feats)
            heads[spot, :] = own[:, :128]
            tails[spot, :] = jnp.concatenate([own[:, 128:], own[:, 128:]], axis=1)
        return carry

    lax.fori_loop(0, feats // 2, pair, 0)
    count = rows // 2 * feats
    for rel, out in enumerate((mine, other)):
        out[0:count, :] = heads[rel * count : (rel + 1) * count, :].astype(BF)
        first = tails[rel * count : rel * count + count // 2, 0:TAIL]
        second = tails[rel * count + count // 2 : (rel + 1) * count, TAIL:128]
        out[count:, :] = jnp.concatenate([first, second], axis=1).astype(BF)


def finish_kernel(rows, feats, mine, theirs, out):
    me = lax.axis_index("feat")
    core = lax.rem(lax.axis_index("rows"), 2)
    share = rows // 4
    count = rows * feats

    def whole(ref, k):
        n = share * feats
        part = k // 2
        tail = ref[count + (k % 2) * n : count + (k % 2 + 1) * n, :]
        x = jnp.concatenate([ref[k * n : (k + 1) * n, :], halves(tail, part)], axis=1)
        return x.reshape(share, feats, WIDTH)

    for first in range(2):

        @pl.when(core == first)
        def _():
            for k in range(4):
                start = lax.rem(me + k, 4) * share
                out[pl.ds(start, share), first * feats : (first + 1) * feats, :] = whole(mine, k)
                out[pl.ds(start, share), (1 - first) * feats : (2 - first) * feats, :] = whole(theirs, k)


def spot_of(y, x, z, c):
    return ((y * 4 + x) * 2 + z) * 2 + c


def moves(change):
    return [
        (spot_of(y, x, z, c), spot_of(*change(y, x, z, c)))
        for y in range(4)
        for x in range(4)
        for z in range(2)
        for c in range(2)
    ]


def moves_both(change):
    return [
        (spot_of(y, x, z, c) * 4 + f, (lambda t: spot_of(*t[0]) * 4 + t[1])(change((y, x, z, c), f)))
        for y in range(4)
        for x in range(4)
        for z in range(2)
        for c in range(2)
        for f in range(4)
    ]


def along(shift, first):
    def change(y, x, z, c):
        if (c == 0) == first:
            return (y, (x + shift) % 4, z, c)
        return ((y + shift) % 4, x, z, c)

    return moves(change)


def local(
    cells,
    labels,
    missing,
    feat_qkv,
    feat_out,
    gain_feat,
    row_q,
    row_kv,
    row_out,
    gain_row,
    mlp_in,
    mlp_out,
    gain_mlp,
):
    rows, feats, width = cells.shape
    share = rows // 4
    half = feats // 2
    gain_feat, gain_row, gain_mlp = (g.reshape(1, width) for g in (gain_feat, gain_row, gain_mlp))

    def shape(n):
        return jax.ShapeDtypeStruct((n, 128), BF)

    main_n = share * feats * 3 // 2 + share
    train_n = TRAIN_MOST * feats * 3 // 2 + 16
    *mains, train = pl.pallas_call(
        functools.partial(prepare_kernel, rows, feats),
        out_shape=[shape(main_n)] * 4 + [shape(train_n)],
        in_specs=[VMEM, SMEM, VMEM],
        out_specs=[VMEM] * 5,
        scratch_shapes=[pltpu.VMEM((TRAIN_MOST, feats, width), BF), pltpu.VMEM((16, 128), F32)],
        name="prepare",
        **params(0, 2 * cells.size * 2),
    )(cells, labels, missing)

    def turn(array, k):
        return lax.ppermute(array, "feat", [(f, (f + k) % 4) for f in range(4)])

    trains = [train] + [turn(train, k) for k in (1, 2, 3)]
    *trains, mains = lax.optimization_barrier((*trains, tuple(mains)))
    mains = [mains[0]] + [turn(mains[k], k) for k in (1, 2, 3)]

    weights = (feat_qkv, feat_out, gain_feat)
    scratch = [pltpu.VMEM((2 * width, width), BF), pltpu.VMEM((2, width, HEADS * 128), BF)]
    piece_n = half * TRAIN_MOST * 3 // 2 + 16
    own, away = pl.pallas_call(
        functools.partial(train_kernel, feats),
        out_shape=[shape(piece_n)] * 2,
        in_specs=[VMEM] * 8,
        out_specs=[VMEM] * 2,
        scratch_shapes=scratch
        + [pltpu.VMEM((feats * TRAIN_MOST, 128), F32), pltpu.VMEM((feats * TRAIN_MOST, 128), F32)],
        name="train_rows",
        **params(2 * 10**9, 10**6, 10**6),
    )(*trains, labels.reshape(1, rows), *weights)
    near = [
        lax.ppermute(own, "rows", moves(lambda y, x, z, c: (y, x, 1 - z, c))),
        lax.ppermute(away, "rows", moves(lambda y, x, z, c: (y, x, z, 1 - c))),
        lax.ppermute(away, "rows", moves(lambda y, x, z, c: (y, x, 1 - z, 1 - c))),
    ]
    train_each = 4 * TRAIN_MOST
    group_n = half * train_each * 3 // 2 + train_each
    group = pl.pallas_call(
        functools.partial(merge_kernel, half),
        out_shape=shape(group_n),
        in_specs=[VMEM] * 4,
        out_specs=VMEM,
        name="merge",
        **params(0, 10**6),
    )(own, *near)
    line = jnp.concatenate(
        [group] + [lax.ppermute(group, "rows", along(k, True)) for k in (1, 2, 3)], axis=0
    )
    plane = [line] + [lax.ppermute(line, "rows", along(k, False)) for k in (1, 2, 3)]

    chunk_n = half * share * 3 // 2
    pieces = pl.pallas_call(
        functools.partial(feature_kernel, share, feats),
        out_shape=[shape(chunk_n)] * 8,
        in_specs=[VMEM] * 7,
        out_specs=[VMEM] * 8,
        scratch_shapes=scratch
        + [pltpu.VMEM((4 * feats * share, 128), F32), pltpu.VMEM((4 * feats * share, 128), F32)],
        name="features",
        **params(4 * 10**9, 3 * 10**6, 2 * 10**6),
    )(*mains, *weights)

    def back(array, k, cross):
        def change(spot, f):
            y, x, z, c = spot
            return (y, x, z, c ^ cross), (f - k) % 4

        return lax.ppermute(array, ("rows", "feat"), moves_both(change))

    chunks = []
    for cross in range(2):
        for k in range(4):
            array = pieces[2 * k + cross]
            chunks.append(array if k == 0 and cross == 0 else back(array, k, cross))

    out_n = rows * half * 3 // 2
    mine, other = pl.pallas_call(
        functools.partial(row_kernel, half, share, train_each),
        out_shape=[shape(out_n)] * 2,
        in_specs=[VMEM] * 19,
        out_specs=[VMEM] * 2,
        scratch_shapes=[
            pltpu.VMEM((width, width), BF),
            pltpu.VMEM((width, width), BF),
            pltpu.VMEM((2, 256, HEADS * 128), BF),
            pltpu.VMEM((2, 16 * train_each, width), BF),
            pltpu.VMEM((4 * rows, width), BF),
            pltpu.VMEM((16 * train_each, TAIL), BF),
            pltpu.VMEM((2 * rows * half, 128), F32),
            pltpu.VMEM((2 * rows * half, 128), F32),
        ],
        name="rows",
        **params(20 * 10**9, 6 * 10**6, 7 * 10**6),
    )(*plane, *chunks, row_q, row_kv, row_out, gain_row, mlp_in, mlp_out, gain_mlp)
    theirs = lax.ppermute(other, "rows", moves(lambda y, x, z, c: (y, x, z, 1 - c)))
    return pl.pallas_call(
        functools.partial(finish_kernel, rows, half),
        out_shape=jax.ShapeDtypeStruct(cells.shape, BF),
        in_specs=[VMEM] * 2,
        out_specs=VMEM,
        name="finish",
        **params(0, 2 * 10**6),
    )(mine, theirs)


def solution(mesh):
    placed = (
        P("rows", "feat", None),
        P("rows"),
        P("rows", "feat"),
        P(),
        P(),
        P(),
        P(),
        P(),
        P(),
        P(),
        P(),
        P(),
        P(),
    )
    return jax.shard_map(
        local, mesh=mesh, in_specs=placed, out_specs=P("rows", "feat", None), check_vma=False
    )
```

```python
import functools
import math

import jax
import jax.numpy as jnp
from jax import lax
from jax.experimental import pallas as pl
from jax.experimental.pallas import tpu as pltpu
from jax.sharding import PartitionSpec as P

HEADS = 6
HEAD = 32
WIDTH = 192
TAIL = WIDTH - 128
TRAIN_MOST = 8
EPSILON = 1e-05
BF = jnp.bfloat16
F32 = jnp.float32
NEVER = -1e30
SCALE = math.log2(math.e) / math.sqrt(HEAD)
VMEM = pl.BlockSpec(memory_space=pltpu.VMEM)
SMEM = pl.BlockSpec(memory_space=pltpu.SMEM)


def mm(a, b):
    return lax.dot_general(a, b, (((1,), (0,)), ((), ())), preferred_element_type=F32)


def mm_nt(a, b):
    return lax.dot_general(a, b, (((1,), (1,)), ((), ())), preferred_element_type=F32)


def mm_tn(a, b):
    return lax.dot_general(a, b, (((0,), (0,)), ((), ())), preferred_element_type=F32)


def layer_norm(values, gain):
    average = jnp.mean(values, axis=-1, keepdims=True)
    centred = values - average
    variance = jnp.mean(centred * centred, axis=-1, keepdims=True)
    return centred * lax.rsqrt(variance + EPSILON) * gain


def turned(w):
    return jnp.transpose(w.astype(F32)).astype(BF)


def params(flops, size, exps=0):
    return dict(
        compiler_params=pltpu.CompilerParams(vmem_limit_bytes=56 * 2**20),
        cost_estimate=pl.CostEstimate(flops=flops, bytes_accessed=size, transcendentals=exps),
    )


def halves(tail, part):
    return tail[:, part * TAIL : (part + 1) * TAIL]


def missing_columns(turned_missing):
    feats, rows = turned_missing.shape
    flags = jnp.concatenate([turned_missing[...].astype(F32), jnp.zeros((feats, 128 - rows), F32)], axis=1)
    return jnp.transpose(jnp.concatenate([flags, jnp.zeros((128 - feats, 128), F32)], axis=0))


def choose_kernel(rows_dev, feats, cells, labels, turned_missing, train, picked, flags, missing):
    missing[...] = missing_columns(turned_missing)
    picked[...] = jnp.zeros(picked.shape, BF)
    flags[...] = jnp.zeros(flags.shape, F32)

    def step(r, slot):
        is_train = labels[r] == 1

        @pl.when(is_train)
        def _():
            picked[slot] = cells[r]
            flags[pl.ds(slot, 1), :] = missing[pl.ds(r, 1), :]

        return jnp.minimum(slot + is_train.astype(jnp.int32), TRAIN_MOST - 1)

    lax.fori_loop(0, rows_dev, step, jnp.int32(0))
    count = TRAIN_MOST * feats
    x = picked[...].reshape(count, WIDTH)
    train[0:count, :] = x[:, :128]
    train[count : count + count // 2, 0:TAIL] = x[: count // 2, 128:]
    train[count : count + count // 2, TAIL:128] = x[count // 2 :, 128:]
    train[count * 3 // 2 :, :] = flags[...].astype(BF)


def prepare_kernel(rows_dev, feats, cells, turned_missing, out0, out1, out2, out3, missing):
    me = lax.axis_index("feat")
    share = rows_dev // 4
    count = share * feats
    missing[...] = missing_columns(turned_missing)
    for k, out in enumerate((out0, out1, out2, out3)):
        start = lax.rem(me + k, 4) * share
        x = cells[pl.ds(start, share)].reshape(count, WIDTH)
        out[0:count, :] = x[:, :128]
        out[count : count + count // 2, 0:TAIL] = x[: count // 2, 128:]
        out[count : count + count // 2, TAIL:128] = x[count // 2 :, 128:]
        out[count * 3 // 2 :, :] = missing[pl.ds(start, share), :].astype(BF)


def staged(count, stages):
    for step in range(count + len(stages) - 1):
        for lag in reversed(range(len(stages))):
            if 0 <= step - lag < count:
                stages[lag](step - lag)


def feature_scratch(width, all_feats):
    return [
        pltpu.VMEM((2 * width, width), BF),
        pltpu.VMEM((4, 2 * all_feats, width), BF),
        pltpu.VMEM((2, 2 * all_feats, width), BF),
        pltpu.VMEM((4, 2 * width, 2 * all_feats), BF),
        pltpu.VMEM((4, width, HEADS * 128), BF),
        pltpu.VMEM((4, all_feats, HEADS * 128), F32),
        pltpu.VMEM((4, width, all_feats), BF),
    ]


def feature_rows(pieces, rows, feats, weights, scratch, keep, emit):
    feat_qkv, feat_out, gain_feat = weights
    turned_qv, inputs, all_keys, all_qv, blocks, all_scores, mixes = scratch
    all_feats = 4 * feats
    turned_qv[0:WIDTH, :] = turned(feat_qkv[:, 0:WIDTH])
    turned_qv[WIDTH : 2 * WIDTH, :] = turned(feat_qkv[:, 2 * WIDTH : 3 * WIDTH])
    blocks[...] = jnp.zeros(blocks.shape, BF)
    count = rows * feats
    flags = jnp.concatenate([p[count * 3 // 2 :, 0:feats].astype(F32) for p in pieces], axis=1)
    flags = jnp.concatenate([flags, jnp.zeros((128 - flags.shape[0], all_feats), F32)], axis=0)
    flags = jnp.transpose(flags)
    same = lax.broadcasted_iota(jnp.int32, (all_feats, all_feats), 0) == lax.broadcasted_iota(
        jnp.int32, (all_feats, all_feats), 1
    )
    gain = gain_feat[...]

    def project(r):
        for part in range(2):
            row = r + part * (rows // 2)
            for n, p in enumerate(pieces):
                spot = slice(part * all_feats + n * feats, part * all_feats + (n + 1) * feats)
                inputs[r % 4, spot, 0:128] = p[row * feats : (row + 1) * feats, :]
                inputs[r % 4, spot, 128:WIDTH] = halves(
                    p[count + r * feats : count + (r + 1) * feats, :], part
                )
        x = inputs[r % 4]
        all_keys[r % 2] = mm(x, feat_qkv[:, WIDTH : 2 * WIDTH]).astype(BF)
        turned_q_v = mm_nt(turned_qv[...], x).astype(BF)
        all_qv[r % 4] = turned_q_v
        for part in range(2):
            for h in range(HEADS):
                blocks[
                    2 * (r % 2) + part, h * HEAD : (h + 1) * HEAD, h * 128 : h * 128 + 128
                ] = turned_q_v[h * HEAD : (h + 1) * HEAD, part * all_feats : (part + 1) * all_feats]

    def score(r):
        for part in range(2):
            all_scores[2 * (r % 2) + part] = mm(
                all_keys[r % 2, part * all_feats : (part + 1) * all_feats, :],
                blocks[2 * (r % 2) + part],
            )

    def attend(r):
        for part in range(2):
            row = r + part * (rows // 2)
            allowed = (flags[:, row : row + 1] == 0) | same
            scores = all_scores[2 * (r % 2) + part]
            scores = jnp.concatenate(
                [
                    jnp.where(allowed, scores[:, h * 128 : (h + 1) * 128], NEVER)
                    for h in range(HEADS)
                ],
                axis=1,
            )
            highest = jnp.max(scores, axis=0, keepdims=True)
            exps = jnp.exp2((scores - highest) * SCALE)
            total = jnp.sum(exps, axis=0, keepdims=True)
            probs = exps.astype(BF)
            for g in range(HEADS // 2):
                mixed = mm(
                    all_qv[
                        r % 4,
                        WIDTH + g * 64 : WIDTH + (g + 1) * 64,
                        part * all_feats : (part + 1) * all_feats,
                    ],
                    probs[:, g * 256 : (g + 1) * 256],
                )
                for i in range(2):
                    h = 2 * g + i
                    mixes[2 * (r % 2) + part, h * HEAD : (h + 1) * HEAD, :] = (
                        mixed[i * HEAD : (i + 1) * HEAD, i * 128 : (i + 1) * 128]
                        / total[:, h * 128 : (h + 1) * 128]
                    ).astype(BF)

    def close(r):
        for part in range(2):
            update = mm_tn(mixes[2 * (r % 2) + part], feat_out[...])[0:keep]
            x = inputs[r % 4, part * all_feats : part * all_feats + keep, :]
            emit(r + part * (rows // 2), layer_norm(x.astype(F32) + update, gain))

    staged(rows // 2, (project, score, attend, close))


def train_kernel(
    feats, p0, p1, p2, p3, labels, feat_qkv, feat_out, gain_feat, mine, other, *rest
):
    scratch, (heads, tails) = rest[:-2], rest[-2:]
    core = lax.rem(lax.axis_index("rows"), 2)

    def emit(row, y):
        heads[pl.ds(row, feats, stride=TRAIN_MOST), :] = y[:, :128]
        tails[pl.ds(row, feats, stride=TRAIN_MOST), :] = jnp.concatenate([y[:, 128:], y[:, 128:]], axis=1)

    feature_rows(
        (p0, p1, p2, p3), TRAIN_MOST, feats, (feat_qkv, feat_out, gain_feat), scratch, feats, emit
    )
    count = feats // 2 * TRAIN_MOST
    trained = jnp.sum(labels[...], axis=1, keepdims=True)
    bias = jnp.where(lax.broadcasted_iota(jnp.int32, (16, 128), 0) < trained, 0.0, NEVER)
    for rel, out in enumerate((mine, other)):
        base = jnp.where(rel == 0, core, 1 - core) * count
        out[0:count, :] = heads[pl.ds(base, count), :].astype(BF)
        first = tails[pl.ds(base, count // 2), 0:TAIL]
        second = tails[pl.ds(base + count // 2, count // 2), TAIL:128]
        out[count : count * 3 // 2, :] = jnp.concatenate([first, second], axis=1).astype(BF)
        out[count * 3 // 2 :, :] = bias.astype(BF)


def merge_kernel(feats, a, b, c, d, out):
    count = feats * TRAIN_MOST
    parts = [p[...].astype(F32) for p in (a, b, c, d)]

    def side(start, groups):
        joined = jnp.concatenate(
            [p[start : start + groups * 8].reshape(groups, 8, 128) for p in parts], axis=1
        )
        return joined.reshape(groups * 32, 128).astype(BF)

    out[0 : 4 * count, :] = side(0, feats)
    out[4 * count : 6 * count, :] = side(count, feats // 2)
    out[6 * count :, :] = side(count * 3 // 2, 1)


def feature_kernel(rows, feats, p0, p1, p2, p3, feat_qkv, feat_out, gain_feat, out, *rest):
    scratch, (heads, tails) = rest[:-2], rest[-2:]
    core = lax.rem(lax.axis_index("rows"), 2)
    me = lax.axis_index("feat")

    def emit(row, y):
        heads[pl.ds(row, 4 * feats, stride=rows), :] = y[:, :128]
        tails[pl.ds(row, 4 * feats, stride=rows), :] = jnp.concatenate([y[:, 128:], y[:, 128:]], axis=1)

    feature_rows(
        (p0, p1, p2, p3), rows, feats, (feat_qkv, feat_out, gain_feat), scratch, 4 * feats, emit
    )
    count = feats // 2 * rows
    for k in range(4):
        peer = lax.rem(me + 4 - k, 4)
        for rel in range(2):
            base = (2 * k + jnp.where(rel == 0, core, 1 - core)) * count
            spot = (2 * peer + rel) * (count * 3 // 2)
            out[pl.ds(spot, count), :] = heads[pl.ds(base, count), :].astype(BF)
            first = tails[pl.ds(base, count // 2), 0:TAIL]
            second = tails[pl.ds(base + count // 2, count // 2), TAIL:128]
            out[pl.ds(spot + count, count // 2), :] = jnp.concatenate([first, second], axis=1).astype(BF)


def row_scratch(rows, feats, keys_all, width):
    return [
        pltpu.VMEM((2 * width, width), BF),
        pltpu.VMEM((2, keys_all, width), BF),
        pltpu.VMEM((4, rows, width), BF),
        pltpu.VMEM((2, keys_all, 256), BF),
        pltpu.VMEM((4, width, keys_all), BF),
        pltpu.VMEM((2, 256, HEADS * 128), BF),
        pltpu.VMEM((2, keys_all, HEADS * 128), F32),
        pltpu.VMEM((2, width, rows), BF),
        pltpu.VMEM((2, rows, width), BF),
        pltpu.VMEM((rows * feats, 128), F32),
        pltpu.VMEM((rows * feats, 128), F32),
    ]


def row_kernel(feats, share, train_each, *refs):
    trains, chunks = refs[0:4], refs[4:6]
    row_q, row_kv, row_out, gain_row, mlp_in, mlp_out, gain_mlp = refs[6:13]
    mine, other = refs[13:15]
    turned_qv, train_cells, inputs, all_keys, all_values, blocks, all_scores, mixes, middles, heads, tails = refs[15:]
    rows = share * 8
    chunk_n = feats * share * 3 // 2
    chunks = [(chunks[0], 2 * k * chunk_n) for k in range(4)] + [(chunks[1], k * chunk_n) for k in range(4)]
    piece = feats * train_each * 3 // 2 + train_each
    lines = trains[0].shape[0] // piece
    turned_qv[0:WIDTH, :] = turned(row_q[...])
    turned_qv[WIDTH : 2 * WIDTH, :] = turned(row_kv[:, WIDTH : 2 * WIDTH])
    blocks[...] = jnp.zeros(blocks.shape, BF)
    blocks[:, WIDTH : WIDTH + 16, :] = jnp.where(
        lax.broadcasted_iota(jnp.int32, (2, 16, HEADS * 128), 1) == 0, 1.0, 0.0
    ).astype(BF)
    for n in range(4):
        for line in range(lines):
            spot = (n * lines + line) * train_each
            for slot in range(2):
                all_keys[slot, spot : spot + train_each, 128:256] = trains[n][
                    line * piece + feats * train_each * 3 // 2 : (line + 1) * piece, :
                ]

    def project(i, u):
        part, j = u % 2, 2 * i + u // 2
        cells = train_cells.at[u % 2]
        for n in range(4):
            for line in range(lines):
                spot = slice((n * lines + line) * train_each, (n * lines + line + 1) * train_each)
                base = line * piece
                cells[spot, 0:128] = trains[n][
                    pl.ds(base + (j + part * (feats // 2)) * train_each, train_each), :
                ]
                cells[spot, 128:WIDTH] = halves(
                    trains[n][pl.ds(base + feats * train_each + j * train_each, train_each), :], part
                )
        for n, (chunk, base) in enumerate(chunks):
            spot = slice(n * share, (n + 1) * share)
            inputs[u, spot, 0:128] = chunk[pl.ds(base + (j + part * (feats // 2)) * share, share), :]
            inputs[u, spot, 128:WIDTH] = halves(
                chunk[pl.ds(base + feats * share + j * share, share), :], part
            )
        all_keys[u % 2, :, 0:WIDTH] = mm(cells[...], row_kv[:, 0:WIDTH]).astype(BF)
        all_values[u] = mm_nt(turned_qv[WIDTH : 2 * WIDTH, :], cells[...]).astype(BF)
        queries = mm_nt(turned_qv[0:WIDTH, :], inputs[u]).astype(BF)
        for h in range(HEADS):
            blocks[u % 2, h * HEAD : (h + 1) * HEAD, h * 128 : h * 128 + 128] = queries[
                h * HEAD : (h + 1) * HEAD, :
            ]

    def score(i, u):
        all_scores[u % 2] = mm(all_keys[u % 2], blocks[u % 2])

    def attend(i, u):
        scores = all_scores[u % 2]
        highest = jnp.max(scores, axis=0, keepdims=True)
        exps = jnp.exp2((scores - highest) * SCALE)
        total = jnp.sum(exps, axis=0, keepdims=True)
        probs = exps.astype(BF)
        for g in range(HEADS // 2):
            mixed = mm(all_values[u, g * 64 : (g + 1) * 64, :], probs[:, g * 256 : (g + 1) * 256])
            for k in range(2):
                h = 2 * g + k
                mixes[u % 2, h * HEAD : (h + 1) * HEAD, :] = (
                    mixed[k * HEAD : (k + 1) * HEAD, k * 128 : (k + 1) * 128]
                    / total[:, h * 128 : (h + 1) * 128]
                ).astype(BF)

    def close(i, u):
        merged = inputs[u].astype(F32) + mm_tn(mixes[u % 2], row_out[...])
        middles[u % 2] = layer_norm(merged, gain_row[...]).astype(BF)

    def forward(i, u):
        after_rows = middles[u % 2]
        hidden = jax.nn.gelu(mm(after_rows, mlp_in[...])).astype(BF)
        combined = after_rows.astype(F32) + mm_nt(hidden, mlp_out[...])
        y = layer_norm(combined, gain_mlp[...])
        spot = pl.ds(2 * i + u // 2 + (u % 2) * (feats // 2), rows, stride=feats)
        heads[spot, :] = y[:, :128]
        tails[spot, :] = jnp.concatenate([y[:, 128:], y[:, 128:]], axis=1)

    stages = (project, score, attend, close, forward)
    for step in range(4):
        for lag in reversed(range(step + 1)):
            stages[lag](0, step - lag)

    def steps(i, carry):
        for u in range(4):
            for lag in reversed(range(5)):
                stages[lag](i - (u < lag), (u - lag) % 4)
        return carry

    lax.fori_loop(1, feats // 4, steps, 0)
    last = feats // 4 - 1
    for step in range(4):
        for lag in reversed(range(step + 1, 5)):
            stages[lag](last, step - lag + 4)

    count = rows // 2 * feats
    for rel, out in enumerate((mine, other)):
        out[0:count, :] = heads[rel * count : (rel + 1) * count, :].astype(BF)
        first = tails[rel * count : rel * count + count // 2, 0:TAIL]
        second = tails[rel * count + count // 2 : (rel + 1) * count, TAIL:128]
        out[count:, :] = jnp.concatenate([first, second], axis=1).astype(BF)


def finish_kernel(rows, feats, mine, theirs, out):
    core = lax.rem(lax.axis_index("rows"), 2)
    share = rows // 4
    count = rows * feats

    def whole(ref, k):
        n = share * feats
        part = k // 2
        tail = ref[count + (k % 2) * n : count + (k % 2 + 1) * n, :]
        x = jnp.concatenate([ref[k * n : (k + 1) * n, :], halves(tail, part)], axis=1)
        return x.reshape(share, feats, WIDTH)

    for first in range(2):

        @pl.when(core == first)
        def _():
            for k in range(4):
                spot = slice(k * share, (k + 1) * share)
                out[spot, first * feats : (first + 1) * feats, :] = whole(mine, k)
                out[spot, (1 - first) * feats : (2 - first) * feats, :] = whole(theirs, k)


def spot_of(y, x, z, c):
    return ((y * 4 + x) * 2 + z) * 2 + c


def moves(change):
    return [
        (spot_of(y, x, z, c), spot_of(*change(y, x, z, c)))
        for y in range(4)
        for x in range(4)
        for z in range(2)
        for c in range(2)
    ]


def along(shift, first):
    def change(y, x, z, c):
        if (c == 0) == first:
            return (y, (x + shift) % 4, z, c)
        return ((y + shift) % 4, x, z, c)

    return moves(change)


def local(
    cells,
    labels,
    missing,
    feat_qkv,
    feat_out,
    gain_feat,
    row_q,
    row_kv,
    row_out,
    gain_row,
    mlp_in,
    mlp_out,
    gain_mlp,
):
    rows, feats, width = cells.shape
    share = rows // 4
    half = feats // 2
    gain_feat, gain_row, gain_mlp = (g.reshape(1, width) for g in (gain_feat, gain_row, gain_mlp))

    def shape(n):
        return jax.ShapeDtypeStruct((n, 128), BF)

    main_n = share * feats * 3 // 2 + share
    train_n = TRAIN_MOST * feats * 3 // 2 + 16
    turned_missing = missing.T
    train = pl.pallas_call(
        functools.partial(choose_kernel, rows, feats),
        out_shape=shape(train_n),
        in_specs=[VMEM, SMEM, VMEM],
        out_specs=VMEM,
        scratch_shapes=[
            pltpu.VMEM((TRAIN_MOST, feats, width), BF),
            pltpu.VMEM((16, 128), F32),
            pltpu.VMEM((128, 128), F32),
        ],
        name="choose",
        **params(0, cells.size * 2),
    )(cells, labels, turned_missing)
    mains = pl.pallas_call(
        functools.partial(prepare_kernel, rows, feats),
        out_shape=[shape(main_n)] * 4,
        in_specs=[VMEM] * 2,
        out_specs=[VMEM] * 4,
        scratch_shapes=[pltpu.VMEM((128, 128), F32)],
        name="prepare",
        **params(0, 2 * cells.size * 2),
    )(cells, turned_missing)

    def turn(array, k):
        return lax.ppermute(array, "feat", [(f, (f + k) % 4) for f in range(4)])

    trains = [train] + [turn(train, k) for k in (1, 2, 3)]
    two = turn(mains[2], 2)
    mains = [mains[0], turn(mains[1], 1), two, turn(mains[3], 3)]

    weights = (feat_qkv, feat_out, gain_feat)
    scratch = feature_scratch(width, 4 * feats)
    piece_n = half * TRAIN_MOST * 3 // 2 + 16
    own, away = pl.pallas_call(
        functools.partial(train_kernel, feats),
        out_shape=[shape(piece_n)] * 2,
        in_specs=[VMEM] * 8,
        out_specs=[VMEM] * 2,
        scratch_shapes=scratch
        + [pltpu.VMEM((feats * TRAIN_MOST, 128), F32), pltpu.VMEM((feats * TRAIN_MOST, 128), F32)],
        name="train_rows",
        **params(2 * 10**9, 10**6, 10**6),
    )(*trains, labels.reshape(1, rows), *weights)
    near = [
        lax.ppermute(own, "rows", moves(lambda y, x, z, c: (y, x, 1 - z, c))),
        lax.ppermute(away, "rows", moves(lambda y, x, z, c: (y, x, z, 1 - c))),
        lax.ppermute(away, "rows", moves(lambda y, x, z, c: (y, x, 1 - z, 1 - c))),
    ]
    own, near, mains = lax.optimization_barrier((own, near, mains))
    train_each = 4 * TRAIN_MOST
    group_n = half * train_each * 3 // 2 + train_each
    group = pl.pallas_call(
        functools.partial(merge_kernel, half),
        out_shape=shape(group_n),
        in_specs=[VMEM] * 4,
        out_specs=VMEM,
        name="merge",
        **params(0, 10**6),
    )(own, *near)
    line = jnp.concatenate(
        [group] + [lax.ppermute(group, "rows", along(k, True)) for k in (1, 2, 3)], axis=0
    )

    chunk_n = half * share * 3 // 2
    pieces = pl.pallas_call(
        functools.partial(feature_kernel, share, feats),
        out_shape=shape(8 * chunk_n),
        in_specs=[VMEM] * 7,
        out_specs=VMEM,
        scratch_shapes=scratch
        + [pltpu.VMEM((4 * feats * share, 128), F32), pltpu.VMEM((4 * feats * share, 128), F32)],
        name="features",
        **params(4 * 10**9, 3 * 10**6, 2 * 10**6),
    )(*mains, *weights)

    pieces, line = lax.optimization_barrier((pieces, line))
    plane = [line] + [lax.ppermute(line, "rows", along(k, False)) for k in (1, 2, 3)]
    chunks = lax.all_to_all(pieces, "feat", split_axis=0, concat_axis=0, tiled=True)
    crossing = jnp.concatenate(
        [chunks[(2 * k + 1) * chunk_n : (2 * k + 2) * chunk_n] for k in range(4)], axis=0
    )
    chunks = [chunks, lax.ppermute(crossing, "rows", moves(lambda y, x, z, c: (y, x, z, 1 - c)))]

    out_n = rows * half * 3 // 2
    mine, other = pl.pallas_call(
        functools.partial(row_kernel, half, share, train_each),
        out_shape=[shape(out_n)] * 2,
        in_specs=[VMEM] * 13,
        out_specs=[VMEM] * 2,
        scratch_shapes=row_scratch(2 * rows, half, 16 * train_each, width),
        name="rows",
        **params(20 * 10**9, 6 * 10**6, 7 * 10**6),
    )(*plane, *chunks, row_q, row_kv, row_out, gain_row, mlp_in, mlp_out.T, gain_mlp)
    theirs = lax.ppermute(other, "rows", moves(lambda y, x, z, c: (y, x, z, 1 - c)))
    return pl.pallas_call(
        functools.partial(finish_kernel, rows, half),
        out_shape=jax.ShapeDtypeStruct(cells.shape, BF),
        in_specs=[VMEM] * 2,
        out_specs=VMEM,
        name="finish",
        **params(0, 2 * 10**6),
    )(mine, theirs)


def solution(mesh):
    placed = (
        P("rows", "feat", None),
        P("rows"),
        P("rows", "feat"),
        P(),
        P(),
        P(),
        P(),
        P(),
        P(),
        P(),
        P(),
        P(),
        P(),
    )
    return jax.shard_map(
        local, mesh=mesh, in_specs=placed, out_specs=P("rows", "feat", None), check_vma=False
    )
```

```python
import functools
import math

import jax
import jax.numpy as jnp
from jax import lax
from jax.experimental import pallas as pl
from jax.experimental.pallas import tpu as pltpu
from jax.sharding import PartitionSpec as P

HEADS = 6
SHIFTS = (0, 2, 1, 3)
HEAD = 32
WIDTH = 192
TAIL = WIDTH - 128
TRAIN_MOST = 8
EPSILON = 1e-05
BF = jnp.bfloat16
F32 = jnp.float32
NEVER = -1e30
SCALE = math.log2(math.e) / math.sqrt(HEAD)
VMEM = pl.BlockSpec(memory_space=pltpu.VMEM)
SMEM = pl.BlockSpec(memory_space=pltpu.SMEM)


def mm(a, b):
    return lax.dot_general(a, b, (((1,), (0,)), ((), ())), preferred_element_type=F32)


def mm_nt(a, b):
    return lax.dot_general(a, b, (((1,), (1,)), ((), ())), preferred_element_type=F32)


def mm_tn(a, b):
    return lax.dot_general(a, b, (((0,), (0,)), ((), ())), preferred_element_type=F32)


def layer_norm(values, gain):
    average = jnp.mean(values, axis=-1, keepdims=True)
    centred = values - average
    variance = jnp.mean(centred * centred, axis=-1, keepdims=True)
    return centred * lax.rsqrt(variance + EPSILON) * gain


def turned(w):
    return jnp.transpose(w.astype(F32)).astype(BF)


def layer_norm_down(values, gain):
    average = jnp.mean(values, axis=0, keepdims=True)
    centred = values - average
    variance = jnp.mean(centred * centred, axis=0, keepdims=True)
    return centred * lax.rsqrt(variance + EPSILON) * gain


def identity(n):
    return (
        lax.broadcasted_iota(jnp.int32, (n, n), 0) == lax.broadcasted_iota(jnp.int32, (n, n), 1)
    ).astype(F32).astype(BF)


def gain_columns(gain):
    return jnp.transpose(jnp.broadcast_to(gain[...], (128, WIDTH)))


def params(flops, size, exps=0):
    return dict(
        compiler_params=pltpu.CompilerParams(vmem_limit_bytes=56 * 2**20),
        cost_estimate=pl.CostEstimate(flops=flops, bytes_accessed=size, transcendentals=exps),
    )


def halves(tail, part):
    return tail[:, part * TAIL : (part + 1) * TAIL]


def missing_columns(turned_missing):
    feats, rows = turned_missing.shape
    flags = jnp.concatenate([turned_missing[...].astype(F32), jnp.zeros((feats, 128 - rows), F32)], axis=1)
    return jnp.transpose(jnp.concatenate([flags, jnp.zeros((128 - feats, 128), F32)], axis=0))


def choose_kernel(rows_dev, feats, cells, labels, turned_missing, train, picked, flags, missing):
    missing[...] = missing_columns(turned_missing)
    picked[...] = jnp.zeros(picked.shape, BF)
    flags[...] = jnp.zeros(flags.shape, F32)

    def step(r, slot):
        is_train = labels[r] == 1

        @pl.when(is_train)
        def _():
            picked[slot] = cells[r]
            flags[pl.ds(slot, 1), :] = missing[pl.ds(r, 1), :]

        return jnp.minimum(slot + is_train.astype(jnp.int32), TRAIN_MOST - 1)

    lax.fori_loop(0, rows_dev, step, jnp.int32(0))
    count = TRAIN_MOST * feats
    x = picked[...].reshape(count, WIDTH)
    train[0:count, :] = x[:, :128]
    train[count : count + count // 2, 0:TAIL] = x[: count // 2, 128:]
    train[count : count + count // 2, TAIL:128] = x[count // 2 :, 128:]
    train[count * 3 // 2 :, :] = flags[...].astype(BF)


def prepare_kernel(rows_dev, feats, cells, turned_missing, out0, out1, out2, out3, missing):
    me = lax.axis_index("feat")
    share = rows_dev // 4
    count = share * feats
    missing[...] = missing_columns(turned_missing)
    for k, out in enumerate((out0, out1, out2, out3)):
        start = lax.rem(me + k, 4) * share
        x = cells[pl.ds(start, share)].reshape(count, WIDTH)
        out[0:count, :] = x[:, :128]
        out[count : count + count // 2, 0:TAIL] = x[: count // 2, 128:]
        out[count : count + count // 2, TAIL:128] = x[count // 2 :, 128:]
        out[count * 3 // 2 :, :] = missing[pl.ds(start, share), :].astype(BF)


def staged(count, stages):
    for step in range(count + len(stages) - 1):
        for lag in reversed(range(len(stages))):
            if 0 <= step - lag < count:
                stages[lag](step - lag)


def feature_scratch(width, all_feats):
    return [
        pltpu.VMEM((3 * width, width), BF),
        pltpu.VMEM((width, width), BF),
        pltpu.VMEM((all_feats, all_feats), BF),
        pltpu.VMEM((width, 2 * all_feats), F32),
        pltpu.VMEM((2, 2 * all_feats, width), BF),
        pltpu.VMEM((2, 2 * all_feats, width), BF),
        pltpu.VMEM((4, 3 * width, 2 * all_feats), BF),
        pltpu.VMEM((4, width, HEADS * 128), BF),
        pltpu.VMEM((4, all_feats, HEADS * 128), F32),
        pltpu.VMEM((2, width, 2 * all_feats), BF),
        pltpu.VMEM((2, width, 2 * all_feats), BF),
    ]


def feature_rows(pieces, rows, feats, weights, scratch, keep, emit):
    feat_qkv, feat_out, gain_feat = weights
    turned_qv, turned_out, same_lanes, gains, inputs, all_keys, all_qv, blocks, all_scores, mixes, results = scratch
    all_feats = 4 * feats
    turned_qv[0:WIDTH, :] = turned(feat_qkv[:, 0:WIDTH])
    turned_qv[WIDTH : 2 * WIDTH, :] = turned(feat_qkv[:, 2 * WIDTH : 3 * WIDTH])
    turned_qv[2 * WIDTH : 3 * WIDTH, :] = identity(WIDTH)
    turned_out[...] = turned(feat_out[...])
    same_lanes[...] = identity(all_feats)
    gains[...] = jnp.concatenate([gain_columns(gain_feat)] * 2, axis=1)
    blocks[...] = jnp.zeros(blocks.shape, BF)
    count = rows * feats
    flags = jnp.concatenate([p[count * 3 // 2 :, 0:feats].astype(F32) for p in pieces], axis=1)
    flags = jnp.concatenate([flags, jnp.zeros((128 - flags.shape[0], all_feats), F32)], axis=0)
    flags = jnp.transpose(flags)
    same = lax.broadcasted_iota(jnp.int32, (all_feats, all_feats), 0) == lax.broadcasted_iota(
        jnp.int32, (all_feats, all_feats), 1
    )

    def project(r):
        for part in range(2):
            row = r + part * (rows // 2)
            for n, p in enumerate(pieces):
                spot = slice(part * all_feats + n * feats, part * all_feats + (n + 1) * feats)
                inputs[r % 2, spot, 0:128] = p[row * feats : (row + 1) * feats, :]
                inputs[r % 2, spot, 128:WIDTH] = halves(
                    p[count + r * feats : count + (r + 1) * feats, :], part
                )
        x = inputs[r % 2]
        all_keys[r % 2] = mm(x, feat_qkv[:, WIDTH : 2 * WIDTH]).astype(BF)
        turned_q_v = mm_nt(turned_qv[...], x).astype(BF)
        all_qv[r % 4] = turned_q_v
        for part in range(2):
            for h in range(HEADS):
                blocks[
                    2 * (r % 2) + part, h * HEAD : (h + 1) * HEAD, h * 128 : h * 128 + 128
                ] = turned_q_v[h * HEAD : (h + 1) * HEAD, part * all_feats : (part + 1) * all_feats]

    def score(r):
        for part in range(2):
            all_scores[2 * (r % 2) + part] = mm(
                all_keys[r % 2, part * all_feats : (part + 1) * all_feats, :],
                blocks[2 * (r % 2) + part],
            )

    def attend(r):
        for part in range(2):
            row = r + part * (rows // 2)
            allowed = (flags[:, row : row + 1] == 0) | same
            scores = all_scores[2 * (r % 2) + part]
            scores = jnp.concatenate(
                [
                    jnp.where(allowed, scores[:, h * 128 : (h + 1) * 128], NEVER)
                    for h in range(HEADS)
                ],
                axis=1,
            )
            highest = jnp.max(scores, axis=0, keepdims=True)
            exps = jnp.exp2((scores - highest) * SCALE)
            total = jnp.sum(exps, axis=0, keepdims=True)
            probs = exps.astype(BF)
            for g in range(HEADS // 2):
                mixed = mm(
                    all_qv[
                        r % 4,
                        WIDTH + g * 64 : WIDTH + (g + 1) * 64,
                        part * all_feats : (part + 1) * all_feats,
                    ],
                    probs[:, g * 256 : (g + 1) * 256],
                )
                for i in range(2):
                    h = 2 * g + i
                    mixes[
                        r % 2, h * HEAD : (h + 1) * HEAD, part * all_feats : (part + 1) * all_feats
                    ] = (
                        mixed[i * HEAD : (i + 1) * HEAD, i * 128 : (i + 1) * 128]
                        / total[:, h * 128 : (h + 1) * 128]
                    ).astype(BF)

    def close(r):
        merged = all_qv[r % 4, 2 * WIDTH : 3 * WIDTH, :].astype(F32) + mm(turned_out[...], mixes[r % 2])
        results[r % 2] = layer_norm_down(merged, gains[...]).astype(BF)

    def turn_back(r):
        for part in range(2):
            y = results[r % 2, :, part * all_feats : (part + 1) * all_feats]
            emit(r + part * (rows // 2), mm_nt(same_lanes[...], y)[0:keep])

    staged(rows // 2, (project, score, attend, close, turn_back))


def train_kernel(
    feats, p0, p1, p2, p3, labels, feat_qkv, feat_out, gain_feat, mine, other, *rest
):
    scratch, (heads, tails) = rest[:-2], rest[-2:]
    core = lax.rem(lax.axis_index("rows"), 2)

    def emit(row, y):
        heads[pl.ds(row, feats, stride=TRAIN_MOST), :] = y[:, :128]
        tails[pl.ds(row, feats, stride=TRAIN_MOST), :] = jnp.concatenate([y[:, 128:], y[:, 128:]], axis=1)

    feature_rows(
        (p0, p1, p2, p3), TRAIN_MOST, feats, (feat_qkv, feat_out, gain_feat), scratch, feats, emit
    )
    count = feats // 2 * TRAIN_MOST
    trained = jnp.sum(labels[...], axis=1, keepdims=True)
    bias = jnp.where(lax.broadcasted_iota(jnp.int32, (16, 128), 0) < trained, 0.0, NEVER)
    for rel, out in enumerate((mine, other)):
        base = jnp.where(rel == 0, core, 1 - core) * count
        out[0:count, :] = heads[pl.ds(base, count), :].astype(BF)
        first = tails[pl.ds(base, count // 2), 0:TAIL]
        second = tails[pl.ds(base + count // 2, count // 2), TAIL:128]
        out[count : count * 3 // 2, :] = jnp.concatenate([first, second], axis=1).astype(BF)
        out[count * 3 // 2 :, :] = bias.astype(BF)


def merge_kernel(feats, a, b, c, d, out):
    count = feats * TRAIN_MOST
    parts = [p[...].astype(F32) for p in (a, b, c, d)]

    def side(start, groups):
        joined = jnp.concatenate(
            [p[start : start + groups * 8].reshape(groups, 8, 128) for p in parts], axis=1
        )
        return joined.reshape(groups * 32, 128).astype(BF)

    out[0 : 4 * count, :] = side(0, feats)
    out[4 * count : 6 * count, :] = side(count, feats // 2)
    out[6 * count :, :] = side(count * 3 // 2, 1)


def feature_kernel(rows, feats, p0, p1, p2, p3, feat_qkv, feat_out, gain_feat, out, *rest):
    scratch, (heads, tails) = rest[:-2], rest[-2:]
    core = lax.rem(lax.axis_index("rows"), 2)
    me = lax.axis_index("feat")

    def emit(row, y):
        heads[pl.ds(row, 4 * feats, stride=rows), :] = y[:, :128]
        tails[pl.ds(row, 4 * feats, stride=rows), :] = jnp.concatenate([y[:, 128:], y[:, 128:]], axis=1)

    feature_rows(
        (p0, p1, p2, p3), rows, feats, (feat_qkv, feat_out, gain_feat), scratch, 4 * feats, emit
    )
    count = feats // 2 * rows
    for k in range(4):
        peer = lax.rem(me + 4 - SHIFTS[k], 4)
        for rel in range(2):
            base = (2 * k + jnp.where(rel == 0, core, 1 - core)) * count
            spot = (2 * peer + rel) * (count * 3 // 2)
            out[pl.ds(spot, count), :] = heads[pl.ds(base, count), :].astype(BF)
            first = tails[pl.ds(base, count // 2), 0:TAIL]
            second = tails[pl.ds(base + count // 2, count // 2), TAIL:128]
            out[pl.ds(spot + count, count // 2), :] = jnp.concatenate([first, second], axis=1).astype(BF)


def row_scratch(rows, feats, keys_all, width):
    return [
        pltpu.VMEM((2 * width, width), BF),
        pltpu.VMEM((2, keys_all, width), BF),
        pltpu.VMEM((4, rows, width), BF),
        pltpu.VMEM((2, keys_all, 256), BF),
        pltpu.VMEM((4, width, keys_all), BF),
        pltpu.VMEM((2, 256, HEADS * 128), BF),
        pltpu.VMEM((2, keys_all, HEADS * 128), F32),
        pltpu.VMEM((2, width, rows), BF),
        pltpu.VMEM((2, rows, width), BF),
        pltpu.VMEM((rows * feats, 128), F32),
        pltpu.VMEM((rows * feats, 128), F32),
    ]


def row_kernel(feats, share, train_each, *refs):
    trains, chunks = refs[0:4], refs[4:6]
    row_q, row_kv, row_out, gain_row, mlp_in, mlp_out, gain_mlp = refs[6:13]
    mine, other = refs[13:15]
    turned_qv, train_cells, inputs, all_keys, all_values, blocks, all_scores, mixes, middles, heads, tails = refs[15:]
    rows = share * 8
    chunk_n = feats * share * 3 // 2
    chunks = [(chunks[0], 2 * k * chunk_n) for k in range(4)] + [(chunks[1], k * chunk_n) for k in range(4)]
    piece = feats * train_each * 3 // 2 + train_each
    lines = trains[0].shape[0] // piece
    turned_qv[0:WIDTH, :] = turned(row_q[...])
    turned_qv[WIDTH : 2 * WIDTH, :] = turned(row_kv[:, WIDTH : 2 * WIDTH])
    blocks[...] = jnp.zeros(blocks.shape, BF)
    blocks[:, WIDTH : WIDTH + 16, :] = jnp.where(
        lax.broadcasted_iota(jnp.int32, (2, 16, HEADS * 128), 1) == 0, 1.0, 0.0
    ).astype(BF)
    for n in range(4):
        for line in range(lines):
            spot = (n * lines + line) * train_each
            for slot in range(2):
                all_keys[slot, spot : spot + train_each, 128:256] = trains[n][
                    line * piece + feats * train_each * 3 // 2 : (line + 1) * piece, :
                ]

    def project(i, u):
        part, j = u % 2, 2 * i + u // 2
        cells = train_cells.at[u % 2]
        for n in range(4):
            for line in range(lines):
                spot = slice((n * lines + line) * train_each, (n * lines + line + 1) * train_each)
                base = line * piece
                cells[spot, 0:128] = trains[n][
                    pl.ds(base + (j + part * (feats // 2)) * train_each, train_each), :
                ]
                cells[spot, 128:WIDTH] = halves(
                    trains[n][pl.ds(base + feats * train_each + j * train_each, train_each), :], part
                )
        for n, (chunk, base) in enumerate(chunks):
            spot = slice(n * share, (n + 1) * share)
            inputs[u, spot, 0:128] = chunk[pl.ds(base + (j + part * (feats // 2)) * share, share), :]
            inputs[u, spot, 128:WIDTH] = halves(
                chunk[pl.ds(base + feats * share + j * share, share), :], part
            )
        all_keys[u % 2, :, 0:WIDTH] = mm(cells[...], row_kv[:, 0:WIDTH]).astype(BF)
        all_values[u] = mm_nt(turned_qv[WIDTH : 2 * WIDTH, :], cells[...]).astype(BF)
        queries = mm_nt(turned_qv[0:WIDTH, :], inputs[u]).astype(BF)
        for h in range(HEADS):
            blocks[u % 2, h * HEAD : (h + 1) * HEAD, h * 128 : h * 128 + 128] = queries[
                h * HEAD : (h + 1) * HEAD, :
            ]

    def score(i, u):
        all_scores[u % 2] = mm(all_keys[u % 2], blocks[u % 2])

    def attend(i, u):
        scores = all_scores[u % 2]
        highest = jnp.max(scores, axis=0, keepdims=True)
        exps = jnp.exp2((scores - highest) * SCALE)
        total = jnp.sum(exps, axis=0, keepdims=True)
        probs = exps.astype(BF)
        for g in range(HEADS // 2):
            mixed = mm(all_values[u, g * 64 : (g + 1) * 64, :], probs[:, g * 256 : (g + 1) * 256])
            for k in range(2):
                h = 2 * g + k
                mixes[u % 2, h * HEAD : (h + 1) * HEAD, :] = (
                    mixed[k * HEAD : (k + 1) * HEAD, k * 128 : (k + 1) * 128]
                    / total[:, h * 128 : (h + 1) * 128]
                ).astype(BF)

    def close(i, u):
        merged = inputs[u].astype(F32) + mm_tn(mixes[u % 2], row_out[...])
        middles[u % 2] = layer_norm(merged, gain_row[...]).astype(BF)

    def forward(i, u):
        after_rows = middles[u % 2]
        hidden = jax.nn.gelu(mm(after_rows, mlp_in[...])).astype(BF)
        combined = after_rows.astype(F32) + mm_nt(hidden, mlp_out[...])
        y = layer_norm(combined, gain_mlp[...])
        spot = pl.ds(2 * i + u // 2 + (u % 2) * (feats // 2), rows, stride=feats)
        heads[spot, :] = y[:, :128]
        tails[spot, :] = jnp.concatenate([y[:, 128:], y[:, 128:]], axis=1)

    stages = (project, score, attend, close, forward)
    for step in range(4):
        for lag in reversed(range(step + 1)):
            stages[lag](0, step - lag)

    def steps(i, carry):
        for u in range(4):
            for lag in reversed(range(5)):
                stages[lag](i - (u < lag), (u - lag) % 4)
        return carry

    lax.fori_loop(1, feats // 4, steps, 0)
    last = feats // 4 - 1
    for step in range(4):
        for lag in reversed(range(step + 1, 5)):
            stages[lag](last, step - lag + 4)

    count = rows // 2 * feats
    for rel, out in enumerate((mine, other)):
        out[0:count, :] = heads[rel * count : (rel + 1) * count, :].astype(BF)
        first = tails[rel * count : rel * count + count // 2, 0:TAIL]
        second = tails[rel * count + count // 2 : (rel + 1) * count, TAIL:128]
        out[count:, :] = jnp.concatenate([first, second], axis=1).astype(BF)


def finish_kernel(rows, feats, mine, theirs, out):
    core = lax.rem(lax.axis_index("rows"), 2)
    share = rows // 4
    count = rows * feats

    def whole(ref, k):
        n = share * feats
        part = k // 2
        tail = ref[count + (k % 2) * n : count + (k % 2 + 1) * n, :]
        x = jnp.concatenate([ref[k * n : (k + 1) * n, :], halves(tail, part)], axis=1)
        return x.reshape(share, feats, WIDTH)

    for first in range(2):

        @pl.when(core == first)
        def _():
            for k in range(4):
                spot = slice(k * share, (k + 1) * share)
                out[spot, first * feats : (first + 1) * feats, :] = whole(mine, k)
                out[spot, (1 - first) * feats : (2 - first) * feats, :] = whole(theirs, k)


def spot_of(y, x, z, c):
    return ((y * 4 + x) * 2 + z) * 2 + c


def moves(change):
    return [
        (spot_of(y, x, z, c), spot_of(*change(y, x, z, c)))
        for y in range(4)
        for x in range(4)
        for z in range(2)
        for c in range(2)
    ]


def along(shift, first):
    def change(y, x, z, c):
        if (c == 0) == first:
            return (y, (x + shift) % 4, z, c)
        return ((y + shift) % 4, x, z, c)

    return moves(change)


def local(
    cells,
    labels,
    missing,
    feat_qkv,
    feat_out,
    gain_feat,
    row_q,
    row_kv,
    row_out,
    gain_row,
    mlp_in,
    mlp_out,
    gain_mlp,
):
    rows, feats, width = cells.shape
    share = rows // 4
    half = feats // 2
    gain_feat, gain_row, gain_mlp = (g.reshape(1, width) for g in (gain_feat, gain_row, gain_mlp))

    def shape(n):
        return jax.ShapeDtypeStruct((n, 128), BF)

    main_n = share * feats * 3 // 2 + share
    train_n = TRAIN_MOST * feats * 3 // 2 + 16
    turned_missing = missing.T
    train = pl.pallas_call(
        functools.partial(choose_kernel, rows, feats),
        out_shape=shape(train_n),
        in_specs=[VMEM, SMEM, VMEM],
        out_specs=VMEM,
        scratch_shapes=[
            pltpu.VMEM((TRAIN_MOST, feats, width), BF),
            pltpu.VMEM((16, 128), F32),
            pltpu.VMEM((128, 128), F32),
        ],
        name="choose",
        **params(0, cells.size * 2),
    )(cells, labels, turned_missing)
    mains = pl.pallas_call(
        functools.partial(prepare_kernel, rows, feats),
        out_shape=[shape(main_n)] * 4,
        in_specs=[VMEM] * 2,
        out_specs=[VMEM] * 4,
        scratch_shapes=[pltpu.VMEM((128, 128), F32)],
        name="prepare",
        **params(0, 2 * cells.size * 2),
    )(cells, turned_missing)

    def turn(array, k):
        return lax.ppermute(array, "feat", [(f, (f + k) % 4) for f in range(4)])

    trains = [train] + [turn(train, k) for k in (1, 3, 2)]
    mains = [mains[0]] + [turn(mains[k], k) for k in SHIFTS[1:]]

    weights = (feat_qkv, feat_out, gain_feat)
    scratch = feature_scratch(width, 4 * feats)
    piece_n = half * TRAIN_MOST * 3 // 2 + 16
    own, away = pl.pallas_call(
        functools.partial(train_kernel, feats),
        out_shape=[shape(piece_n)] * 2,
        in_specs=[VMEM] * 8,
        out_specs=[VMEM] * 2,
        scratch_shapes=scratch
        + [pltpu.VMEM((feats * TRAIN_MOST, 128), F32), pltpu.VMEM((feats * TRAIN_MOST, 128), F32)],
        name="train_rows",
        **params(2 * 10**9, 10**6, 10**6),
    )(*trains, labels.reshape(1, rows), *weights)
    near = [
        lax.ppermute(own, "rows", moves(lambda y, x, z, c: (y, x, 1 - z, c))),
        lax.ppermute(away, "rows", moves(lambda y, x, z, c: (y, x, z, 1 - c))),
        lax.ppermute(away, "rows", moves(lambda y, x, z, c: (y, x, 1 - z, 1 - c))),
    ]
    own, near, mains = lax.optimization_barrier((own, near, mains))
    train_each = 4 * TRAIN_MOST
    group_n = half * train_each * 3 // 2 + train_each
    group = pl.pallas_call(
        functools.partial(merge_kernel, half),
        out_shape=shape(group_n),
        in_specs=[VMEM] * 4,
        out_specs=VMEM,
        name="merge",
        **params(0, 10**6),
    )(own, *near)
    far = lax.ppermute(group, "rows", along(2, True))
    line = jnp.concatenate(
        [group] + [lax.ppermute(group, "rows", along(k, True)) for k in (1, 3)] + [far], axis=0
    )

    chunk_n = half * share * 3 // 2
    pieces = pl.pallas_call(
        functools.partial(feature_kernel, share, feats),
        out_shape=shape(8 * chunk_n),
        in_specs=[VMEM] * 7,
        out_specs=VMEM,
        scratch_shapes=scratch
        + [pltpu.VMEM((4 * feats * share, 128), F32), pltpu.VMEM((4 * feats * share, 128), F32)],
        name="features",
        **params(4 * 10**9, 3 * 10**6, 2 * 10**6),
    )(*mains, *weights)

    pieces, line = lax.optimization_barrier((pieces, line))
    far = lax.ppermute(line, "rows", along(2, False))
    plane = [line] + [lax.ppermute(line, "rows", along(k, False)) for k in (1, 3)] + [far]
    chunks = lax.all_to_all(pieces, "feat", split_axis=0, concat_axis=0, tiled=True)
    crossing = jnp.concatenate(
        [chunks[(2 * k + 1) * chunk_n : (2 * k + 2) * chunk_n] for k in range(4)], axis=0
    )
    chunks = [chunks, lax.ppermute(crossing, "rows", moves(lambda y, x, z, c: (y, x, z, 1 - c)))]

    out_n = rows * half * 3 // 2
    mine, other = pl.pallas_call(
        functools.partial(row_kernel, half, share, train_each),
        out_shape=[shape(out_n)] * 2,
        in_specs=[VMEM] * 13,
        out_specs=[VMEM] * 2,
        scratch_shapes=row_scratch(2 * rows, half, 16 * train_each, width),
        name="rows",
        **params(20 * 10**9, 6 * 10**6, 7 * 10**6),
    )(*plane, *chunks, row_q, row_kv, row_out, gain_row, mlp_in, mlp_out.T, gain_mlp)
    theirs = lax.ppermute(other, "rows", moves(lambda y, x, z, c: (y, x, z, 1 - c)))
    return pl.pallas_call(
        functools.partial(finish_kernel, rows, half),
        out_shape=jax.ShapeDtypeStruct(cells.shape, BF),
        in_specs=[VMEM] * 2,
        out_specs=VMEM,
        name="finish",
        **params(0, 2 * 10**6),
    )(mine, theirs)


def solution(mesh):
    placed = (
        P("rows", "feat", None),
        P("rows"),
        P("rows", "feat"),
        P(),
        P(),
        P(),
        P(),
        P(),
        P(),
        P(),
        P(),
        P(),
        P(),
    )
    return jax.shard_map(
        local, mesh=mesh, in_specs=placed, out_specs=P("rows", "feat", None), check_vma=False
    )
```

```python
import functools
import math

import jax
import jax.numpy as jnp
from jax import lax
from jax.experimental import pallas as pl
from jax.experimental.pallas import tpu as pltpu
from jax.sharding import PartitionSpec as P

HEADS = 6
SHIFTS = (0, 2, 1, 3)
HEAD = 32
WIDTH = 192
TAIL = WIDTH - 128
TRAIN_MOST = 8
EPSILON = 1e-05
BF = jnp.bfloat16
F32 = jnp.float32
NEVER = -1e30
SCALE = math.log2(math.e) / math.sqrt(HEAD)
VMEM = pl.BlockSpec(memory_space=pltpu.VMEM)
SMEM = pl.BlockSpec(memory_space=pltpu.SMEM)


def mm(a, b):
    return lax.dot_general(a, b, (((1,), (0,)), ((), ())), preferred_element_type=F32)


def mm_nt(a, b):
    return lax.dot_general(a, b, (((1,), (1,)), ((), ())), preferred_element_type=F32)


def mm_tn(a, b):
    return lax.dot_general(a, b, (((0,), (0,)), ((), ())), preferred_element_type=F32)


def layer_norm(values, gain):
    average = jnp.mean(values, axis=-1, keepdims=True)
    centred = values - average
    variance = jnp.mean(centred * centred, axis=-1, keepdims=True)
    return centred * lax.rsqrt(variance + EPSILON) * gain


def turned(w):
    return jnp.transpose(w.astype(F32)).astype(BF)


def layer_norm_down(values, gain):
    average = jnp.mean(values, axis=0, keepdims=True)
    centred = values - average
    variance = jnp.mean(centred * centred, axis=0, keepdims=True)
    return centred * lax.rsqrt(variance + EPSILON) * gain


def identity(n):
    return (
        lax.broadcasted_iota(jnp.int32, (n, n), 0) == lax.broadcasted_iota(jnp.int32, (n, n), 1)
    ).astype(F32).astype(BF)


def gain_columns(gain):
    return jnp.transpose(jnp.broadcast_to(gain[...], (128, WIDTH)))


def params(flops, size, exps=0):
    return dict(
        compiler_params=pltpu.CompilerParams(vmem_limit_bytes=56 * 2**20),
        cost_estimate=pl.CostEstimate(flops=flops, bytes_accessed=size, transcendentals=exps),
    )


def halves(tail, part):
    return tail[:, part * TAIL : (part + 1) * TAIL]


def missing_columns(turned_missing):
    feats, rows = turned_missing.shape
    flags = jnp.concatenate([turned_missing[...].astype(F32), jnp.zeros((feats, 128 - rows), F32)], axis=1)
    return jnp.transpose(jnp.concatenate([flags, jnp.zeros((128 - feats, 128), F32)], axis=0))


def place(rows_dev, labels, order):
    trained = lax.fori_loop(0, rows_dev, lambda r, n: n + labels[r], jnp.int32(0), unroll=16)

    def step(r, carry):
        train, test = carry
        is_train = labels[r] == 1
        slot = jnp.where(is_train, train, trained + test)
        order[jnp.clip(slot, 0, rows_dev - 1)] = r
        one = is_train.astype(jnp.int32)
        return train + one, test + 1 - one

    lax.fori_loop(0, rows_dev, step, (jnp.int32(0), jnp.int32(0)), unroll=8)


def choose_kernel(rows_dev, feats, cells, labels, turned_missing, train, order, picked, flags, missing):
    missing[...] = missing_columns(turned_missing)
    flags[...] = jnp.zeros(flags.shape, F32)

    place(rows_dev, labels, order)
    for slot in range(TRAIN_MOST):
        picked[slot] = cells[order[slot]]
        flags[slot : slot + 1, :] = missing[pl.ds(order[slot], 1), :]
    count = TRAIN_MOST * feats
    x = picked[...].reshape(count, WIDTH)
    train[0:count, :] = x[:, :128]
    train[count : count + count // 2, 0:TAIL] = x[: count // 2, 128:]
    train[count : count + count // 2, TAIL:128] = x[count // 2 :, 128:]
    train[count * 3 // 2 :, :] = flags[...].astype(BF)


def prepare_kernel(
    rows_dev, feats, cells, order, turned_missing, out0, out1, out2, out3, placed, absent, missing
):
    me = lax.axis_index("feat")
    share = (rows_dev - TRAIN_MOST) // 4
    count = share * feats
    missing[...] = missing_columns(turned_missing)
    absent[...] = jnp.zeros(absent.shape, F32)

    for rest in range(rows_dev - TRAIN_MOST):
        row = order[TRAIN_MOST + rest]
        placed[rest] = cells[row]
        spot = rest // share * 16 + rest % share
        absent[spot : spot + 1, :] = missing[pl.ds(row, 1), :]
    for k, out in enumerate((out0, out1, out2, out3)):
        peer = lax.rem(me + k, 4)
        x = placed[pl.ds(peer * share, share)].reshape(count, WIDTH)
        out[0:count, :] = x[:, :128]
        out[count : count * 3 // 2, 0:TAIL] = x[: count // 2, 128:]
        out[count : count * 3 // 2, TAIL:128] = x[count // 2 :, 128:]
        out[count * 3 // 2 :, :] = absent[pl.ds(peer * 16, 16), :].astype(BF)


def staged(count, stages):
    for step in range(count + len(stages) - 1):
        for lag in reversed(range(len(stages))):
            if 0 <= step - lag < count:
                stages[lag](step - lag)


def feature_scratch(width, all_feats):
    return [
        pltpu.VMEM((3 * width, width), BF),
        pltpu.VMEM((width, width), BF),
        pltpu.VMEM((all_feats, all_feats), BF),
        pltpu.VMEM((width, 2 * all_feats), F32),
        pltpu.VMEM((2, 2 * all_feats, width), BF),
        pltpu.VMEM((2, 2 * all_feats, width), BF),
        pltpu.VMEM((4, 3 * width, 2 * all_feats), BF),
        pltpu.VMEM((4, width, HEADS * 128), BF),
        pltpu.VMEM((4, all_feats, HEADS * 128), F32),
        pltpu.VMEM((2, width, 2 * all_feats), BF),
        pltpu.VMEM((2, width, 2 * all_feats), BF),
    ]


def feature_rows(pieces, rows, feats, weights, scratch, keep, emit):
    feat_qkv, feat_out, gain_feat = weights
    turned_qv, turned_out, same_lanes, gains, inputs, all_keys, all_qv, blocks, all_scores, mixes, results = scratch
    all_feats = 4 * feats
    turned_qv[0:WIDTH, :] = turned(feat_qkv[:, 0:WIDTH])
    turned_qv[WIDTH : 2 * WIDTH, :] = turned(feat_qkv[:, 2 * WIDTH : 3 * WIDTH])
    turned_qv[2 * WIDTH : 3 * WIDTH, :] = identity(WIDTH)
    turned_out[...] = turned(feat_out[...])
    same_lanes[...] = identity(all_feats)
    gains[...] = jnp.concatenate([gain_columns(gain_feat)] * 2, axis=1)
    blocks[...] = jnp.zeros(blocks.shape, BF)
    count = rows * feats
    flags = jnp.concatenate([p[count * 3 // 2 :, 0:feats].astype(F32) for p in pieces], axis=1)
    flags = jnp.concatenate([flags, jnp.zeros((128 - flags.shape[0], all_feats), F32)], axis=0)
    flags = jnp.transpose(flags)
    same = lax.broadcasted_iota(jnp.int32, (all_feats, all_feats), 0) == lax.broadcasted_iota(
        jnp.int32, (all_feats, all_feats), 1
    )

    def project(r):
        for part in range(2):
            row = r + part * (rows // 2)
            for n, p in enumerate(pieces):
                spot = slice(part * all_feats + n * feats, part * all_feats + (n + 1) * feats)
                inputs[r % 2, spot, 0:128] = p[row * feats : (row + 1) * feats, :]
                inputs[r % 2, spot, 128:WIDTH] = halves(
                    p[count + r * feats : count + (r + 1) * feats, :], part
                )
        x = inputs[r % 2]
        all_keys[r % 2] = mm(x, feat_qkv[:, WIDTH : 2 * WIDTH]).astype(BF)
        turned_q_v = mm_nt(turned_qv[...], x).astype(BF)
        all_qv[r % 4] = turned_q_v
        for part in range(2):
            for h in range(HEADS):
                blocks[
                    2 * (r % 2) + part, h * HEAD : (h + 1) * HEAD, h * 128 : h * 128 + 128
                ] = turned_q_v[h * HEAD : (h + 1) * HEAD, part * all_feats : (part + 1) * all_feats]

    def score(r):
        for part in range(2):
            all_scores[2 * (r % 2) + part] = mm(
                all_keys[r % 2, part * all_feats : (part + 1) * all_feats, :],
                blocks[2 * (r % 2) + part],
            )

    def attend(r):
        for part in range(2):
            row = r + part * (rows // 2)
            allowed = (flags[:, row : row + 1] == 0) | same
            scores = all_scores[2 * (r % 2) + part]
            scores = jnp.concatenate(
                [
                    jnp.where(allowed, scores[:, h * 128 : (h + 1) * 128], NEVER)
                    for h in range(HEADS)
                ],
                axis=1,
            )
            highest = jnp.max(scores, axis=0, keepdims=True)
            exps = jnp.exp2((scores - highest) * SCALE)
            total = jnp.sum(exps, axis=0, keepdims=True)
            probs = exps.astype(BF)
            for g in range(HEADS // 2):
                mixed = mm(
                    all_qv[
                        r % 4,
                        WIDTH + g * 64 : WIDTH + (g + 1) * 64,
                        part * all_feats : (part + 1) * all_feats,
                    ],
                    probs[:, g * 256 : (g + 1) * 256],
                )
                for i in range(2):
                    h = 2 * g + i
                    mixes[
                        r % 2, h * HEAD : (h + 1) * HEAD, part * all_feats : (part + 1) * all_feats
                    ] = (
                        mixed[i * HEAD : (i + 1) * HEAD, i * 128 : (i + 1) * 128]
                        / total[:, h * 128 : (h + 1) * 128]
                    ).astype(BF)

    def close(r):
        merged = all_qv[r % 4, 2 * WIDTH : 3 * WIDTH, :].astype(F32) + mm(turned_out[...], mixes[r % 2])
        results[r % 2] = layer_norm_down(merged, gains[...]).astype(BF)

    def turn_back(r):
        for part in range(2):
            y = results[r % 2, :, part * all_feats : (part + 1) * all_feats]
            emit(r + part * (rows // 2), mm_nt(same_lanes[...], y)[0:keep])

    staged(rows // 2, (project, score, attend, close, turn_back))


def write_rows(out, spot, heads, tails, base, half):
    rows = heads.shape[0]
    count, middle = rows * half, rows // 2
    out[pl.ds(spot, count), :] = heads[:, pl.ds(base, half), :].reshape(count, 128).astype(BF)
    first = tails[0:middle, pl.ds(base, half), 0:TAIL].reshape(count // 2, TAIL)
    second = tails[middle:rows, pl.ds(base, half), TAIL:128].reshape(count // 2, TAIL)
    out[pl.ds(spot + count, count // 2), :] = jnp.concatenate([first, second], axis=1).astype(BF)


def train_kernel(
    feats, p0, p1, p2, p3, labels, feat_qkv, feat_out, gain_feat, mine, other, kept, lent, *rest
):
    scratch, (heads, tails, rows_heads, rows_tails) = rest[:-4], rest[-4:]
    core = lax.rem(lax.axis_index("rows"), 2)

    def emit(row, y):
        heads[pl.ds(row, feats, stride=TRAIN_MOST), :] = y[:, :128]
        twice = jnp.concatenate([y[:, 128:], y[:, 128:]], axis=1)
        tails[pl.ds(row, feats, stride=TRAIN_MOST), :] = twice
        rows_heads[row] = y[:, :128]
        rows_tails[row] = twice

    feature_rows(
        (p0, p1, p2, p3), TRAIN_MOST, feats, (feat_qkv, feat_out, gain_feat), scratch, feats, emit
    )
    count = feats // 2 * TRAIN_MOST
    trained = jnp.sum(labels[...], axis=1, keepdims=True)
    bias = jnp.where(lax.broadcasted_iota(jnp.int32, (16, 128), 0) < trained, 0.0, NEVER)
    for rel, out in enumerate((mine, other)):
        base = jnp.where(rel == 0, core, 1 - core) * count
        out[0:count, :] = heads[pl.ds(base, count), :].astype(BF)
        first = tails[pl.ds(base, count // 2), 0:TAIL]
        second = tails[pl.ds(base + count // 2, count // 2), TAIL:128]
        out[count : count * 3 // 2, :] = jnp.concatenate([first, second], axis=1).astype(BF)
        out[count * 3 // 2 :, :] = bias.astype(BF)


    for rel, out in enumerate((kept, lent)):
        base = jnp.where(rel == 0, core, 1 - core) * (feats // 2)
        write_rows(out, 0, rows_heads, rows_tails, base, feats // 2)


def merge_kernel(feats, a, b, c, d, out):
    count = feats * TRAIN_MOST
    parts = [p[...].astype(F32) for p in (a, b, c, d)]

    def side(start, groups):
        joined = jnp.concatenate(
            [p[start : start + groups * 8].reshape(groups, 8, 128) for p in parts], axis=1
        )
        return joined.reshape(groups * 32, 128).astype(BF)

    out[0 : 4 * count, :] = side(0, feats)
    out[4 * count : 6 * count, :] = side(count, feats // 2)
    out[6 * count :, :] = side(count * 3 // 2, 1)


def feature_kernel(rows, feats, p0, p1, p2, p3, feat_qkv, feat_out, gain_feat, out, *rest):
    scratch, (heads, tails) = rest[:-2], rest[-2:]
    core = lax.rem(lax.axis_index("rows"), 2)
    me = lax.axis_index("feat")

    def emit(row, y):
        heads[row] = y[:, :128]
        tails[row] = jnp.concatenate([y[:, 128:], y[:, 128:]], axis=1)

    feature_rows(
        (p0, p1, p2, p3), rows, feats, (feat_qkv, feat_out, gain_feat), scratch, 4 * feats, emit
    )
    half = feats // 2
    size = half * rows * 3 // 2
    for k in range(4):
        peer = lax.rem(me + 4 - SHIFTS[k], 4)
        for rel in range(2):
            base = k * feats + jnp.where(rel == 0, core, 1 - core) * half
            write_rows(out, (2 * peer + rel) * size, heads, tails, base, half)


def row_scratch(rows, feats, keys_all, width):
    return [
        pltpu.VMEM((2 * width, width), BF),
        pltpu.VMEM((2, keys_all, width), BF),
        pltpu.VMEM((4, rows, width), BF),
        pltpu.VMEM((2, keys_all, 256), BF),
        pltpu.VMEM((4, width, keys_all), BF),
        pltpu.VMEM((2, 256, HEADS * 128), BF),
        pltpu.VMEM((2, keys_all, HEADS * 128), F32),
        pltpu.VMEM((2, width, rows), BF),
        pltpu.VMEM((2, rows, width), BF),
        pltpu.VMEM((rows * feats, 128), F32),
        pltpu.VMEM((rows * feats, 128), F32),
        pltpu.VMEM((rows * feats, 128), F32),
        pltpu.VMEM((rows * feats, 128), F32),
    ]


def row_kernel(feats, share, train_each, *refs):
    trains, (inner, kept, crossed) = refs[0:4], refs[4:7]
    row_q, row_kv, row_out, gain_row, mlp_in, mlp_out, gain_mlp = refs[7:14]
    mine, other = refs[14:16]
    turned_qv, train_cells, inputs, all_keys, all_values, blocks, all_scores, mixes, middles, heads, tails, row_heads, row_tails = refs[16:]
    rows = 2 * (4 * share + TRAIN_MOST)
    size = feats * share * 3 // 2
    parts = [(kept, 0, TRAIN_MOST)] + [(inner, 2 * k * size, share) for k in range(4)]
    parts += [(crossed, 4 * size, TRAIN_MOST)] + [(crossed, k * size, share) for k in range(4)]
    spot = 0
    for ref, base, held in parts:
        count = held * feats
        row_heads[spot : spot + count, :] = ref[base : base + count, :].astype(F32)
        side = ref[base + count : base + count * 3 // 2, :]
        row_tails[spot : spot + count // 2, 0:TAIL] = halves(side, 0).astype(F32)
        row_tails[spot + count // 2 : spot + count, 0:TAIL] = halves(side, 1).astype(F32)
        spot += count
    piece = feats * train_each * 3 // 2 + train_each
    lines = trains[0].shape[0] // piece
    turned_qv[0:WIDTH, :] = turned(row_q[...])
    turned_qv[WIDTH : 2 * WIDTH, :] = turned(row_kv[:, WIDTH : 2 * WIDTH])
    blocks[...] = jnp.zeros(blocks.shape, BF)
    blocks[:, WIDTH : WIDTH + 16, :] = jnp.where(
        lax.broadcasted_iota(jnp.int32, (2, 16, HEADS * 128), 1) == 0, 1.0, 0.0
    ).astype(BF)
    for n in range(4):
        for line in range(lines):
            spot = (n * lines + line) * train_each
            for slot in range(2):
                all_keys[slot, spot : spot + train_each, 128:256] = trains[n][
                    line * piece + feats * train_each * 3 // 2 : (line + 1) * piece, :
                ]

    def project(i, u):
        part, j = u % 2, 2 * i + u // 2
        cells = train_cells.at[u % 2]
        for n in range(4):
            for line in range(lines):
                spot = slice((n * lines + line) * train_each, (n * lines + line + 1) * train_each)
                base = line * piece
                cells[spot, 0:128] = trains[n][
                    pl.ds(base + (j + part * (feats // 2)) * train_each, train_each), :
                ]
                cells[spot, 128:WIDTH] = halves(
                    trains[n][pl.ds(base + feats * train_each + j * train_each, train_each), :], part
                )
        spot = pl.ds(j + part * (feats // 2), rows, stride=feats)
        inputs[u, :, 0:128] = row_heads[spot, :].astype(BF)
        inputs[u, :, 128:WIDTH] = row_tails[spot, :][:, 0:TAIL].astype(BF)
        all_keys[u % 2, :, 0:WIDTH] = mm(cells[...], row_kv[:, 0:WIDTH]).astype(BF)
        all_values[u] = mm_nt(turned_qv[WIDTH : 2 * WIDTH, :], cells[...]).astype(BF)
        queries = mm_nt(turned_qv[0:WIDTH, :], inputs[u]).astype(BF)
        for h in range(HEADS):
            blocks[u % 2, h * HEAD : (h + 1) * HEAD, h * 128 : h * 128 + 128] = queries[
                h * HEAD : (h + 1) * HEAD, :
            ]

    def score(i, u):
        all_scores[u % 2] = mm(all_keys[u % 2], blocks[u % 2])

    def attend(i, u):
        scores = all_scores[u % 2]
        highest = jnp.max(scores, axis=0, keepdims=True)
        exps = jnp.exp2((scores - highest) * SCALE)
        total = jnp.sum(exps, axis=0, keepdims=True)
        probs = exps.astype(BF)
        for g in range(HEADS // 2):
            mixed = mm(all_values[u, g * 64 : (g + 1) * 64, :], probs[:, g * 256 : (g + 1) * 256])
            for k in range(2):
                h = 2 * g + k
                mixes[u % 2, h * HEAD : (h + 1) * HEAD, :] = (
                    mixed[k * HEAD : (k + 1) * HEAD, k * 128 : (k + 1) * 128]
                    / total[:, h * 128 : (h + 1) * 128]
                ).astype(BF)

    def close(i, u):
        merged = inputs[u].astype(F32) + mm_tn(mixes[u % 2], row_out[...])
        middles[u % 2] = layer_norm(merged, gain_row[...]).astype(BF)

    def forward(i, u):
        after_rows = middles[u % 2]
        hidden = jax.nn.gelu(mm(after_rows, mlp_in[...])).astype(BF)
        combined = after_rows.astype(F32) + mm_nt(hidden, mlp_out[...])
        y = layer_norm(combined, gain_mlp[...])
        spot = pl.ds(2 * i + u // 2 + (u % 2) * (feats // 2), rows, stride=feats)
        heads[spot, :] = y[:, :128]
        tails[spot, :] = jnp.concatenate([y[:, 128:], y[:, 128:]], axis=1)

    stages = (project, score, attend, close, forward)
    for step in range(4):
        for lag in reversed(range(step + 1)):
            stages[lag](0, step - lag)

    def steps(i, carry):
        for u in range(4):
            for lag in reversed(range(5)):
                stages[lag](i - (u < lag), (u - lag) % 4)
        return carry

    lax.fori_loop(1, feats // 4, steps, 0)
    last = feats // 4 - 1
    for step in range(4):
        for lag in reversed(range(step + 1, 5)):
            stages[lag](last, step - lag + 4)

    count = rows // 2 * feats
    for rel, out in enumerate((mine, other)):
        out[0:count, :] = heads[rel * count : (rel + 1) * count, :].astype(BF)
        first = tails[rel * count : rel * count + count // 2, 0:TAIL]
        second = tails[rel * count + count // 2 : (rel + 1) * count, TAIL:128]
        out[count:, :] = jnp.concatenate([first, second], axis=1).astype(BF)


def finish_kernel(rows, feats, mine, theirs, order, out):
    core = lax.rem(lax.axis_index("rows"), 2)
    share = rows // 4
    count = rows * feats

    def whole(ref, k):
        n = share * feats
        part = k // 2
        tail = ref[count + (k % 2) * n : count + (k % 2 + 1) * n, :]
        x = jnp.concatenate([ref[k * n : (k + 1) * n, :], halves(tail, part)], axis=1)
        return x.reshape(share, feats, WIDTH)

    for first in range(2):

        @pl.when(core == first)
        def _():
            for k in range(4):
                one, two = whole(mine, k), whole(theirs, k)
                if first == 1:
                    one, two = two, one
                for i in range(share):
                    row = order[k * share + i]
                    out[row, 0:feats, :] = one[i]
                    out[row, feats : 2 * feats, :] = two[i]


def spot_of(y, x, z, c):
    return ((y * 4 + x) * 2 + z) * 2 + c


def moves(change):
    return [
        (spot_of(y, x, z, c), spot_of(*change(y, x, z, c)))
        for y in range(4)
        for x in range(4)
        for z in range(2)
        for c in range(2)
    ]


def along(shift, first):
    def change(y, x, z, c):
        if (c == 0) == first:
            return (y, (x + shift) % 4, z, c)
        return ((y + shift) % 4, x, z, c)

    return moves(change)


def local(
    cells,
    labels,
    missing,
    feat_qkv,
    feat_out,
    gain_feat,
    row_q,
    row_kv,
    row_out,
    gain_row,
    mlp_in,
    mlp_out,
    gain_mlp,
):
    rows, feats, width = cells.shape
    share = (rows - TRAIN_MOST) // 4
    half = feats // 2
    gain_feat, gain_row, gain_mlp = (g.reshape(1, width) for g in (gain_feat, gain_row, gain_mlp))

    def shape(n):
        return jax.ShapeDtypeStruct((n, 128), BF)

    main_n = share * feats * 3 // 2 + 16
    train_n = TRAIN_MOST * feats * 3 // 2 + 16
    turned_missing = missing.T
    train, order = pl.pallas_call(
        functools.partial(choose_kernel, rows, feats),
        out_shape=[shape(train_n), jax.ShapeDtypeStruct((rows,), jnp.int32)],
        in_specs=[VMEM, SMEM, VMEM],
        out_specs=[VMEM, SMEM],
        scratch_shapes=[
            pltpu.VMEM((TRAIN_MOST, feats, width), BF),
            pltpu.VMEM((16, 128), F32),
            pltpu.VMEM((128, 128), F32),
        ],
        name="choose",
        **params(0, cells.size * 2),
    )(cells, labels, turned_missing)
    mains = pl.pallas_call(
        functools.partial(prepare_kernel, rows, feats),
        out_shape=[shape(main_n)] * 4,
        in_specs=[VMEM, SMEM, VMEM],
        out_specs=[VMEM] * 4,
        scratch_shapes=[
            pltpu.VMEM((rows - TRAIN_MOST, feats, width), BF),
            pltpu.VMEM((64, 128), F32),
            pltpu.VMEM((128, 128), F32),
        ],
        name="prepare",
        **params(0, 2 * cells.size * 2),
    )(cells, order, turned_missing)

    def turn(array, k):
        return lax.ppermute(array, "feat", [(f, (f + k) % 4) for f in range(4)])

    trains = [train] + [turn(train, k) for k in (1, 3, 2)]
    mains = [mains[0]] + [turn(mains[k], k) for k in SHIFTS[1:]]

    weights = (feat_qkv, feat_out, gain_feat)
    scratch = feature_scratch(width, 4 * feats)
    piece_n = half * TRAIN_MOST * 3 // 2 + 16
    own, away, kept, lent = pl.pallas_call(
        functools.partial(train_kernel, feats),
        out_shape=[shape(piece_n)] * 2 + [shape(TRAIN_MOST * half * 3 // 2)] * 2,
        in_specs=[VMEM] * 8,
        out_specs=[VMEM] * 4,
        scratch_shapes=scratch
        + [pltpu.VMEM((feats * TRAIN_MOST, 128), F32)] * 2
        + [pltpu.VMEM((TRAIN_MOST, feats, 128), F32)] * 2,
        name="train_rows",
        **params(2 * 10**9, 10**6, 10**6),
    )(*trains, labels.reshape(1, rows), *weights)
    near = [
        lax.ppermute(own, "rows", moves(lambda y, x, z, c: (y, x, 1 - z, c))),
        lax.ppermute(away, "rows", moves(lambda y, x, z, c: (y, x, z, 1 - c))),
        lax.ppermute(away, "rows", moves(lambda y, x, z, c: (y, x, 1 - z, 1 - c))),
    ]
    own, near, mains = lax.optimization_barrier((own, near, mains))
    train_each = 4 * TRAIN_MOST
    group_n = half * train_each * 3 // 2 + train_each
    group = pl.pallas_call(
        functools.partial(merge_kernel, half),
        out_shape=shape(group_n),
        in_specs=[VMEM] * 4,
        out_specs=VMEM,
        name="merge",
        **params(0, 10**6),
    )(own, *near)
    far = lax.ppermute(group, "rows", along(2, True))
    line = jnp.concatenate(
        [group] + [lax.ppermute(group, "rows", along(k, True)) for k in (1, 3)] + [far], axis=0
    )

    chunk_n = half * share * 3 // 2
    pieces = pl.pallas_call(
        functools.partial(feature_kernel, share, feats),
        out_shape=shape(8 * chunk_n),
        in_specs=[VMEM] * 7,
        out_specs=VMEM,
        scratch_shapes=scratch
        + [pltpu.VMEM((share, 4 * feats, 128), F32)] * 2,
        name="features",
        **params(4 * 10**9, 3 * 10**6, 2 * 10**6),
    )(*mains, *weights)

    pieces, line = lax.optimization_barrier((pieces, line))
    far = lax.ppermute(line, "rows", along(2, False))
    plane = [line] + [lax.ppermute(line, "rows", along(k, False)) for k in (1, 3)] + [far]
    chunks = lax.all_to_all(pieces, "feat", split_axis=0, concat_axis=0, tiled=True)
    crossing = jnp.concatenate(
        [chunks[(2 * k + 1) * chunk_n : (2 * k + 2) * chunk_n] for k in range(4)] + [lent], axis=0
    )
    chunks = [chunks, kept, lax.ppermute(crossing, "rows", moves(lambda y, x, z, c: (y, x, z, 1 - c)))]

    out_n = rows * half * 3 // 2
    mine, other = pl.pallas_call(
        functools.partial(row_kernel, half, share, train_each),
        out_shape=[shape(out_n)] * 2,
        in_specs=[VMEM] * 14,
        out_specs=[VMEM] * 2,
        scratch_shapes=row_scratch(2 * rows, half, 16 * train_each, width),
        name="rows",
        **params(20 * 10**9, 6 * 10**6, 7 * 10**6),
    )(*plane, *chunks, row_q, row_kv, row_out, gain_row, mlp_in, mlp_out.T, gain_mlp)
    theirs = lax.ppermute(other, "rows", moves(lambda y, x, z, c: (y, x, z, 1 - c)))
    return pl.pallas_call(
        functools.partial(finish_kernel, rows, half),
        out_shape=jax.ShapeDtypeStruct(cells.shape, BF),
        in_specs=[VMEM, VMEM, SMEM],
        out_specs=VMEM,
        name="finish",
        **params(0, 2 * 10**6),
    )(mine, theirs, order)


def solution(mesh):
    placed = (
        P("rows", "feat", None),
        P("rows"),
        P("rows", "feat"),
        P(),
        P(),
        P(),
        P(),
        P(),
        P(),
        P(),
        P(),
        P(),
        P(),
    )
    return jax.shard_map(
        local, mesh=mesh, in_specs=placed, out_specs=P("rows", "feat", None), check_vma=False
    )
```
